512 devices in a mesh: ctx: 64 (over z, x), tp: 8 (over y, core).
Axes of the slice: x: 4, y: 4, z: 16, core: 2. Of those that a mesh axis runs over, the one named last changes fastest.
Arguments:
- hidden_in: bfloat16 [64, 8192], P(None, 'ctx'), may hold values from -3 to 3
- attn_gain: float32 [8192], P('ctx'), may hold values from 0.5 to 2
- w_query: bfloat16 [8192, 8192], P('ctx', 'tp'), may hold values from -0.0625 to 0.0625
- key_cache: bfloat16 [32768, 1024], P('ctx', 'tp'), may hold values from -41 to 41
- value_cache: bfloat16 [32768, 1024], P('ctx', 'tp'), may hold values from -6 to 6
- block_lengths: int32 [64], P('ctx'), may hold values from 1 to 512, 24576 in all
- question_length: int32 [1], replicated, may hold values from 32 to 64
- w_out: bfloat16 [8192, 8192], P('tp', 'ctx'), may hold values from -0.0625 to 0.0625
- ffn_gain: float32 [8192], P('ctx'), may hold values from 0.5 to 2
- w_gate: bfloat16 [8192, 14336], P('ctx', 'tp'), may hold values from -0.0625 to 0.0625
- w_up: bfloat16 [8192, 14336], P('ctx', 'tp'), may hold values from -0.0625 to 0.0625
- w_down: bfloat16 [14336, 8192], P('tp', 'ctx'), may hold values from -0.046875 to 0.046875
Outputs:
- layer_out: bfloat16 [64, 8192], P(None, 'ctx')
The draws below stay inside these ranges and needn't reach their ends.
Inputs may be any that keep to these rules, and one draw needn't show every extreme that they name: `block_lengths`: each block has at least one valid token, and some block is full.
All inputs are finite; a program needn't handle non-finite values.
Results may differ from the reference program's by a relative error of at most 0.012.
The reference program's roundings to bfloat16 on the way (of `first_normed`, `queries`, `attended`, `second_normed` and `activated`) count: a program that leaves them out, or rounds other values in their place, can miss the bound.
Values may be sent and summed in bfloat16 or wider, within the bound.
A program may use at most 64 MiB of HBM per device.

```python
import math
import jax
import jax.numpy as jnp
import numpy as np
from jax import lax

D = 8192
HQ = 64
KVH = 8
HD = 128
FF = 14336
QROWS = 64
BLK = 512
GROUPS = 8
CTX = 32768
N_CTX = 64


def draw_key_cache(key, part):
    key = jax.random.fold_in(key, 11)
    first_key = jax.random.fold_in(key, 0)
    shape = (CTX, KVH * HD)
    values = jnp.clip(3.0 * jax.random.normal(first_key, shape, jnp.float32), -15.0, 15.0)
    return values.astype(jnp.bfloat16)


def level_of(stream_key, dims, pieces, low, top_value):
    factor_of, own = 1.0, jax.random.fold_in(stream_key, 6)
    for axis_at, blocks in pieces:
        draws = jnp.exp(jax.random.uniform(jax.random.fold_in(own, axis_at), (blocks,), jnp.float32, low / len(pieces), top_value / len(pieces)))
        factor_of = factor_of * jnp.repeat(draws, dims[axis_at] // blocks).reshape([-1 if axis == axis_at else 1 for axis in range(len(dims))])
    return factor_of


def length_profile(amount, total, reach, lean):
    portions = [(1 << 20) // math.isqrt(grade ** lean) + 1 for grade in range(2, amount + 1)]
    surplus, holding = total - reach - (amount - 1), [1] * (amount - 1)
    while surplus > 0:
        free = [i for i in range(amount - 1) if holding[i] < reach]
        mass, remaining = sum([portions[i] for i in free]), surplus
        for i in free:
            extra = min(reach - holding[i], max(1, remaining * portions[i] // mass), surplus)
            holding[i] = holding[i] + extra
            surplus = surplus - extra
    return np.array([reach] + holding)


def ragged(key, amount, total, reach, skew):
    if amount == 2:
        one = jax.random.randint(key, (), max(1, total - reach), min(reach, total - 1) + 1)
        return jnp.stack([one, total - one])
    tallies = jnp.asarray(length_profile(amount, total, reach, skew), jnp.int32)
    pairs = (amount - 1) // 2
    source_of, taker = tallies[1:1 + 2 * pairs:2], tallies[2:2 + 2 * pairs:2]
    margin = jnp.minimum(source_of - 1, reach - taker)
    shifted = jax.random.randint(jax.random.fold_in(key, 1), (pairs,), 0, 1 << 20) % (margin + 1)
    tallies = tallies.at[1:1 + 2 * pairs:2].set(source_of - shifted).at[2:2 + 2 * pairs:2].set(taker + shifted)
    return tallies[jax.random.permutation(jax.random.fold_in(key, 2), amount)]


def gaussian(own_key, extent, deviation, reach, cuts=(), dtype=jnp.bfloat16):
    values = deviation * jax.random.normal(own_key, extent, jnp.float32)
    if cuts:
        values = values * level_of(own_key, extent, cuts, -0.22, 0.18)
    return jnp.clip(values, -reach, reach).astype(dtype)


def setup_inputs(seed: int = 0) -> dict:
    splits = jax.random.split(jax.random.key(seed), 13)
    hidden_in = gaussian(splits[0], (QROWS, D), 0.5, 3.0, ((1, 64),))
    attn_gain = jnp.clip(jnp.exp(math.log(2.0) - 1.3862944 * jax.random.uniform(splits[1], (D,), jnp.float32) ** level_of(splits[1], (D,), ((0, 64),), -0.2, 0.2)), 0.5, 2.0)
    w_query = gaussian(splits[2], (D, HQ * HD), D ** -0.5, 0.0625, ((0, 64), (1, 8)))
    key_cache = draw_key_cache(jax.random.fold_in(splits[12], 71), 0)
    value_cache = gaussian(splits[4], (CTX, KVH * HD), 1.0, 6.0, ((0, 64), (1, 8)))
    block_lengths = ragged(splits[5], N_CTX, N_CTX * BLK * 3 // 4, BLK, 0).astype(jnp.int32)
    question_length = jax.random.randint(splits[6], (1,), QROWS // 2, QROWS + 1).astype(jnp.int32)
    w_out = gaussian(splits[7], (HQ * HD, D), (HQ * HD) ** -0.5, 0.0625, ((0, 8), (1, 64)))
    ffn_gain = jnp.clip(jnp.exp(math.log(2.0) - 1.3862944 * jax.random.uniform(splits[8], (D,), jnp.float32) ** level_of(splits[8], (D,), ((0, 64),), -0.2, 0.2)), 0.5, 2.0)
    w_gate = gaussian(splits[9], (D, FF), D ** -0.5, 0.0625, ((0, 64), (1, 8)))
    w_up = gaussian(splits[10], (D, FF), D ** -0.5, 0.0625, ((0, 64), (1, 8)))
    w_down = gaussian(splits[11], (FF, D), FF ** -0.5, 0.046875, ((0, 8), (1, 64)))
    return dict(hidden_in=hidden_in, attn_gain=attn_gain, w_query=w_query, key_cache=key_cache, value_cache=value_cache, block_lengths=block_lengths, question_length=question_length, w_out=w_out, ffn_gain=ffn_gain, w_gate=w_gate, w_up=w_up, w_down=w_down)


EPSILON = 1e-05
MASKED = -1e+30

def block_terms(query_heads, keys_block, values_block, length):
    score_scale = 1.0 / math.sqrt(HD)
    scores = jnp.einsum('kgrd,jkd->kgrj', query_heads, keys_block.astype(jnp.float32)) * score_scale
    usable = jnp.arange(BLK) < length
    scores = jnp.where(usable, scores, MASKED)
    maxima = lax.optimization_barrier(jnp.max(scores, axis=3))
    weights = jnp.exp(scores - maxima[..., None])
    totals = lax.optimization_barrier(jnp.sum(weights, axis=3))
    rounded = lax.optimization_barrier(weights.astype(jnp.bfloat16))
    numerators = jnp.einsum('kgrj,jkd->kgrd', rounded.astype(jnp.float32), values_block.astype(jnp.float32))
    return (maxima, totals, numerators)

def reference(hidden_in, attn_gain, w_query, key_cache, value_cache, block_lengths, question_length, w_out, ffn_gain, w_gate, w_up, w_down):
    stream = hidden_in.astype(jnp.float32)
    first_scale = lax.rsqrt(lax.optimization_barrier(jnp.mean(stream * stream, axis=1)) + EPSILON)
    first_normed = (stream * attn_gain).astype(jnp.bfloat16)
    queries = (first_scale[:, None] * jnp.dot(first_normed, w_query, preferred_element_type=jnp.float32)).astype(jnp.bfloat16)
    query_heads = queries.reshape(QROWS, KVH, GROUPS, HD).transpose(1, 2, 0, 3).astype(jnp.float32)
    keys_all = key_cache.reshape(N_CTX, BLK, KVH, HD)
    values_all = value_cache.reshape(N_CTX, BLK, KVH, HD)

    def per_block(operands):
        keys_block, values_block, length = operands
        return block_terms(query_heads, keys_block, values_block, length)
    maxima, totals, numerators = lax.map(per_block, (keys_all, values_all, block_lengths))
    summit = lax.optimization_barrier(jnp.max(maxima, axis=0))
    factor = jnp.exp(maxima - summit[None])
    total = lax.optimization_barrier(jnp.sum(factor * totals, axis=0))
    merged = lax.optimization_barrier(jnp.sum(factor[..., None] * numerators, axis=0))
    attended = (merged / total[..., None]).transpose(2, 0, 1, 3).reshape(QROWS, HQ * HD).astype(jnp.bfloat16)
    residual = stream + jnp.dot(attended, w_out, preferred_element_type=jnp.float32)
    second_scale = lax.rsqrt(lax.optimization_barrier(jnp.mean(residual * residual, axis=1)) + EPSILON)
    second_normed = (residual * ffn_gain).astype(jnp.bfloat16)
    gate = second_scale[:, None] * jnp.dot(second_normed, w_gate, preferred_element_type=jnp.float32)
    up_proj = second_scale[:, None] * jnp.dot(second_normed, w_up, preferred_element_type=jnp.float32)
    activated = (jax.nn.silu(gate) * up_proj).astype(jnp.bfloat16)
    result = residual + jnp.dot(activated, w_down, preferred_element_type=jnp.float32)
    present = jnp.arange(QROWS)[:, None] < question_length[0]
    return jnp.where(present, result, 0.0).astype(jnp.bfloat16)
```

```python
import math

import jax
import jax.numpy as jnp
from jax import lax
from jax.experimental import pallas as pl
from jax.experimental.pallas import tpu as pltpu
from jax.sharding import PartitionSpec as P

D = 8192
HD = 128
EPSILON = 1e-05
MASKED = -1e30
NX = 4
NZ = 16
NT = 8
ROWS = 64
HEAD_CHUNKS = 8
FF_BLOCKS = 14
MESH = pl.DeviceIdType.MESH
F32 = jnp.float32
BF16 = jnp.bfloat16


def lane_row(column):
    shape = (column.shape[0], 128)
    same = lax.broadcasted_iota(jnp.int32, shape, 0) == lax.broadcasted_iota(jnp.int32, shape, 1)
    return jnp.sum(jnp.where(same, jnp.broadcast_to(column, shape), 0.0), axis=0, keepdims=True)


def row_column(row, base):
    shape = (16, 128)
    same = lax.broadcasted_iota(jnp.int32, shape, 0) + base == lax.broadcasted_iota(
        jnp.int32, shape, 1
    )
    return jnp.sum(jnp.where(same, jnp.broadcast_to(row, shape), 0.0), axis=1, keepdims=True)


def kernel(
    length_ref,
    hidden_ref,
    attn_gain_ref,
    ffn_gain_ref,
    wq_hbm,
    key_hbm,
    value_hbm,
    wout_hbm,
    wgate_hbm,
    wup_hbm,
    wdown_hbm,
    out_ref,
    wq,
    key,
    value,
    wout,
    wgate,
    wup,
    wdown,
    load_sems,
    send_sems,
    qx_src,
    qx_dst,
    qz_src,
    qz_dst,
    q_all,
    sx_src,
    sx_dst,
    sz_src,
    sz_dst,
    ax_src,
    ax_dst,
    az_src,
    az_dst,
    a_all,
    tx_src,
    tx_dst,
    tz_src,
    tz_dst,
    p_all,
    fx_src,
    fx_dst,
    fz_src,
    fz_dst,
    f_all,
    ux_src,
    ux_dst,
    uz_src,
    uz_dst,
    d_all,
    recv_sems,
    q_gather_sems,
    a_gather_sems,
    f_gather_sems,
    x_gather_sems,
    p_sems,
    d_sems,
):
    ctx = lax.axis_index("ctx")
    tp = lax.axis_index("tp")
    x = lax.rem(ctx, NX)
    z = lax.div(ctx, NX)

    def x_peer(k):
        return z * NX + lax.rem(x + k, NX)

    def z_peer(k):
        return lax.rem(z + k, NZ) * NX + x

    def t_peer(k):
        return lax.rem(tp + k, NT)

    loads = [
        pltpu.make_async_copy(source, target, load_sems.at[at])
        for at, (source, target) in enumerate(
            [
                (wq_hbm, wq),
                (key_hbm, key),
                (value_hbm, value),
                (wout_hbm, wout),
                (wgate_hbm, wgate),
                (wup_hbm, wup),
                (wdown_hbm, wdown),
            ]
        )
    ]
    for load in loads:
        load.start()

    barrier = pltpu.get_barrier_semaphore()
    for k in range(1, NX):
        pl.semaphore_signal(barrier, inc=1, device_id=(x_peer(k), tp), device_id_type=MESH)
    for k in range(1, NT):
        pl.semaphore_signal(barrier, inc=1, device_id=(ctx, t_peer(k)), device_id_type=MESH)

    def greet(k, carry):
        pl.semaphore_signal(barrier, inc=1, device_id=(z_peer(k), tp), device_id_type=MESH)
        return carry

    lax.fori_loop(1, NZ, greet, 0)

    def send(source, target, send_sem, recv_sem, device):
        pltpu.make_async_remote_copy(
            src_ref=source,
            dst_ref=target,
            send_sem=send_sem,
            recv_sem=recv_sem,
            device_id=device,
            device_id_type=MESH,
        ).start()

    def drain(ref, sem):
        pltpu.make_async_copy(ref, ref, sem).wait()

    stream = hidden_ref[...].astype(F32)
    sx_src[...] = lane_row(jnp.sum(stream * stream, axis=1, keepdims=True))
    normed = (stream * attn_gain_ref[...]).astype(BF16)
    loads[0].wait()
    query_part = jnp.dot(normed, wq[...], preferred_element_type=F32)
    for j in range(NX):
        for h in range(2):
            for g in range(4):
                column = (2 * j + h) * HD
                qx_src[j, 4 * h + g] = query_part[16 * g : 16 * g + 16, column : column + HD]
    pl.semaphore_wait(barrier, NX - 1 + NZ - 1 + NT - 1)

    def x_scatter(source, target, at):
        for k in range(1, NX):
            send(
                source.at[lax.rem(x + k, NX)],
                target.at[k - 1],
                send_sems.at[at],
                recv_sems.at[at],
                (x_peer(k), tp),
            )

    def x_same(source, target, at):
        for k in range(1, NX):
            send(source, target.at[k - 1], send_sems.at[at], recv_sems.at[at], (x_peer(k), tp))

    def reducer_step(count, stride):
        start = lax.div(z + stride - 1, stride)

        def visit(step, body):
            chunk = lax.rem(start + step, count)
            target = chunk * stride
            offset = lax.rem(target - z + NZ, NZ)

            @pl.when(offset != 0)
            def _():
                body(chunk, offset - 1, (target * NX + x, tp))

        return visit

    def z_scatter(source, target, at, row_source, row_target, row_at, count, stride):
        visit = reducer_step(count, stride)

        def step(s, carry):
            def body(chunk, slot, device):
                send(row_source, row_target.at[slot], send_sems.at[row_at], recv_sems.at[row_at], device)
                send(source.at[chunk], target.at[slot], send_sems.at[at], recv_sems.at[at], device)

            visit(s, body)
            return carry

        lax.fori_loop(0, count, step, 0)

    def z_gather(whole, chunk, at, sems):
        def step(k, carry):
            send(
                whole.at[x, chunk],
                whole.at[x, chunk],
                send_sems.at[at],
                sems.at[chunk],
                (z_peer(k), tp),
            )
            return carry

        lax.fori_loop(1, NZ, step, 0)

    def z_gather_wait(whole, sems, count, stride):
        def step(chunk, carry):
            @pl.when(chunk * stride != z)
            def _():
                drain(whole.at[x, chunk], sems.at[chunk])

            return carry

        lax.fori_loop(0, count, step, 0)

    def x_gather(whole, at, sem_at):
        for k in range(1, NX):
            send(
                whole.at[x],
                whole.at[x],
                send_sems.at[at],
                x_gather_sems.at[sem_at + k - 1],
                (x_peer(k), tp),
            )
        for k in range(1, NX):
            drain(whole.at[lax.rem(x + NX - k, NX)], x_gather_sems.at[sem_at + k - 1])

    x_same(sx_src, sx_dst, 0)
    x_scatter(qx_src, qx_dst, 1)
    drain(sx_dst, recv_sems.at[0])
    sz_src[...] = sx_src[...] + sx_dst[0] + sx_dst[1] + sx_dst[2]
    drain(qx_dst, recv_sems.at[1])
    qz_src[...] = qx_src[x] + qx_dst[0] + qx_dst[1] + qx_dst[2]
    z_scatter(qz_src, qz_dst, 3, sz_src, sz_dst, 2, HEAD_CHUNKS, 2)
    even = lax.rem(z, 2) == 0
    half = lax.div(z, 2)

    @pl.when(even)
    def _():
        drain(sz_dst, recv_sems.at[2])
        squares = jnp.sum(sz_dst[...], axis=0) + sz_src[...]
        scale = lax.rsqrt(row_column(squares, 16 * lax.rem(half, 4)) / D + EPSILON)
        drain(qz_dst, recv_sems.at[3])
        total = qz_src[half] + jnp.sum(qz_dst[...], axis=0)
        q_all[x, half] = (scale * total).astype(BF16)
        z_gather(q_all, half, 4, q_gather_sems)

    z_gather_wait(q_all, q_gather_sems, HEAD_CHUNKS, 2)
    x_gather(q_all, 5, 0)

    loads[1].wait()
    loads[2].wait()
    queries = q_all[...].reshape(NX * HEAD_CHUNKS * 16, HD)
    scores = lax.dot_general(
        key[...], queries, (((1,), (1,)), ((), ())), preferred_element_type=F32
    ) * (1.0 / math.sqrt(HD))
    usable = lax.broadcasted_iota(jnp.int32, scores.shape, 0) < length_ref[0]
    scores = jnp.where(usable, scores, MASKED)
    maxima = jnp.max(scores, axis=0, keepdims=True)
    weights = jnp.exp(scores - maxima)
    totals = jnp.sum(weights, axis=0, keepdims=True)
    for j in range(NX):
        tx_src[j, 0] = maxima[:, 128 * j : 128 * j + 128]
        tx_src[j, 1] = totals[:, 128 * j : 128 * j + 128]
    x_scatter(tx_src, tx_dst, 6)
    numerators = lax.dot_general(
        value[...], weights.astype(BF16), (((0,), (0,)), ((), ())), preferred_element_type=F32
    ).astype(BF16)
    for j in range(NX):
        for i in range(HEAD_CHUNKS):
            ax_src[j, i] = numerators[16 * i : 16 * i + 16, 128 * j : 128 * j + 128]
    x_scatter(ax_src, ax_dst, 7)
    drain(tx_dst, recv_sems.at[6])
    pieces = [tx_src.at[x]] + [tx_dst.at[k] for k in range(NX - 1)]
    summit = pieces[0][0]
    for piece in pieces[1:]:
        summit = jnp.maximum(summit, piece[0])
    factors = [jnp.exp(piece[0] - summit) for piece in pieces]
    tz_src[0] = summit
    tz_src[1] = sum(factor * piece[1] for factor, piece in zip(factors, pieces))
    drain(ax_dst, recv_sems.at[7])
    merged = ax_src[x].astype(F32) * factors[0]
    for k in range(NX - 1):
        merged = merged + ax_dst[k].astype(F32) * factors[k + 1]
    az_src[...] = merged.astype(BF16)
    z_scatter(az_src, az_dst, 9, tz_src, tz_dst, 8, HEAD_CHUNKS, 2)

    @pl.when(even)
    def _():
        drain(tz_dst, recv_sems.at[8])
        own = tz_src[0]
        others = tz_dst[:, 0]
        summit = jnp.maximum(own, jnp.max(others, axis=0))
        own_factor = jnp.exp(own - summit)
        factors = jnp.exp(others - summit)
        total = own_factor * tz_src[1] + jnp.sum(factors * tz_dst[:, 1], axis=0)
        drain(az_dst, recv_sems.at[9])
        merged = own_factor * az_src[half].astype(F32) + jnp.sum(
            factors * az_dst[...].astype(F32), axis=0
        )
        a_all[x, half] = (merged / total).astype(BF16)
        z_gather(a_all, half, 10, a_gather_sems)

    z_gather_wait(a_all, a_gather_sems, HEAD_CHUNKS, 2)
    x_gather(a_all, 11, 3)

    loads[3].wait()
    projected = jnp.zeros((ROWS, HD), F32)
    for j in range(NX):
        turned = jnp.transpose(a_all[j].reshape(HD, 128).astype(F32)).astype(BF16)
        for h in range(2):
            at = (2 * j + h) * HD
            projected = projected + jnp.dot(
                turned[ROWS * h : ROWS * h + ROWS],
                wout[at : at + HD],
                preferred_element_type=F32,
            )

    def tp_sum(part, whole, at, sems):
        whole[tp] = part.astype(BF16)
        for k in range(1, NT):
            send(whole.at[tp], whole.at[tp], send_sems.at[at], sems.at[tp], (ctx, t_peer(k)))
        for k in range(1, NT):
            source = t_peer(k)
            drain(whole.at[source], sems.at[source])
        total = whole[0].astype(F32)
        for source in range(1, NT):
            total = total + whole[source].astype(F32)
        return total

    residual = hidden_ref[...].astype(F32) + tp_sum(projected, p_all, 12, p_sems)

    ux_src[...] = lane_row(jnp.sum(residual * residual, axis=1, keepdims=True))
    x_same(ux_src, ux_dst, 13)
    second = (residual * ffn_gain_ref[...]).astype(BF16)
    loads[4].wait()
    loads[5].wait()
    for kind, weight in enumerate((wgate, wup)):
        part = jnp.dot(second, weight[...], preferred_element_type=F32).astype(BF16)
        for j in range(NX):
            for b in range(FF_BLOCKS):
                fx_src[j, b, kind] = part[16 * j : 16 * j + 16, 128 * b : 128 * b + 128]
    x_scatter(fx_src, fx_dst, 14)
    drain(ux_dst, recv_sems.at[13])
    uz_src[...] = ux_src[...] + ux_dst[0] + ux_dst[1] + ux_dst[2]
    drain(fx_dst, recv_sems.at[14])
    fz_src[...] = (
        fx_src[x].astype(F32)
        + fx_dst[0].astype(F32)
        + fx_dst[1].astype(F32)
        + fx_dst[2].astype(F32)
    ).astype(BF16)
    z_scatter(fz_src, fz_dst, 16, uz_src, uz_dst, 15, FF_BLOCKS, 1)

    @pl.when(z < FF_BLOCKS)
    def _():
        drain(uz_dst, recv_sems.at[15])
        squares = jnp.sum(uz_dst[...], axis=0) + uz_src[...]
        scale = lax.rsqrt(row_column(squares, 16 * x) / D + EPSILON)
        drain(fz_dst, recv_sems.at[16])
        both = fz_src[z].astype(F32) + jnp.sum(fz_dst[...].astype(F32), axis=0)
        gate = scale * both[0]
        up = scale * both[1]
        f_all[x, z] = (gate / (1.0 + jnp.exp(-gate)) * up).astype(BF16)
        z_gather(f_all, z, 17, f_gather_sems)

    z_gather_wait(f_all, f_gather_sems, FF_BLOCKS, 1)
    x_gather(f_all, 18, 6)

    loads[6].wait()
    lowered = jnp.zeros((ROWS, HD), F32)
    for b in range(FF_BLOCKS):
        lowered = lowered + jnp.dot(
            f_all[:, b].reshape(ROWS, 128),
            wdown[128 * b : 128 * b + 128],
            preferred_element_type=F32,
        )
    result = residual + tp_sum(lowered, d_all, 19, d_sems)
    out_ref[...] = result.astype(BF16)

    for at, ref in (
        (0, sx_dst),
        (1, qx_dst),
        (5, q_all.at[pl.ds(0, 3)]),
        (6, tx_dst),
        (7, ax_dst),
        (11, a_all.at[pl.ds(0, 3)]),
        (12, p_all.at[pl.ds(0, 7)]),
        (13, ux_dst),
        (14, fx_dst),
        (18, f_all.at[pl.ds(0, 3)]),
        (19, d_all.at[pl.ds(0, 7)]),
    ):
        drain(ref, send_sems.at[at])

    @pl.when(even)
    def _():
        for at, ref in (
            (2, sz_dst),
            (3, qz_dst),
            (8, tz_dst),
            (9, az_dst),
        ):
            drain(ref.at[pl.ds(0, HEAD_CHUNKS - 1)], send_sems.at[at])
        drain(az_dst, send_sems.at[4])
        drain(az_dst, send_sems.at[10])

    @pl.when(jnp.logical_not(even))
    def _():
        for at, ref in (
            (2, sz_dst),
            (3, qz_dst),
            (8, tz_dst),
            (9, az_dst),
        ):
            drain(ref.at[pl.ds(0, HEAD_CHUNKS)], send_sems.at[at])

    @pl.when(z < FF_BLOCKS)
    def _():
        drain(uz_dst.at[pl.ds(0, FF_BLOCKS - 1)], send_sems.at[15])
        drain(fz_dst.at[pl.ds(0, FF_BLOCKS - 1)], send_sems.at[16])
        drain(az_dst, send_sems.at[17])

    @pl.when(z >= FF_BLOCKS)
    def _():
        drain(uz_dst.at[pl.ds(0, FF_BLOCKS)], send_sems.at[15])
        drain(fz_dst.at[pl.ds(0, FF_BLOCKS)], send_sems.at[16])


def body(
    hidden_in,
    attn_gain,
    w_query,
    key_cache,
    value_cache,
    block_lengths,
    question_length,
    w_out,
    ffn_gain,
    w_gate,
    w_up,
    w_down,
):
    vmem = pl.BlockSpec(memory_space=pltpu.VMEM)
    anywhere = pl.BlockSpec(memory_space=pl.ANY)
    weights = (w_query, key_cache, value_cache, w_out, w_gate, w_up, w_down)
    chunk = (16, 128)
    row = (1, 128)
    scratch = [pltpu.VMEM(a.shape, a.dtype) for a in weights]
    scratch += [pltpu.SemaphoreType.DMA((7,)), pltpu.SemaphoreType.DMA((20,))]
    scratch += [
        pltpu.VMEM((NX, HEAD_CHUNKS) + chunk, F32),
        pltpu.VMEM((NX - 1, HEAD_CHUNKS) + chunk, F32),
        pltpu.VMEM((HEAD_CHUNKS,) + chunk, F32),
        pltpu.VMEM((NZ - 1,) + chunk, F32),
        pltpu.VMEM((NX, HEAD_CHUNKS) + chunk, BF16),
        pltpu.VMEM(row, F32),
        pltpu.VMEM((NX - 1,) + row, F32),
        pltpu.VMEM(row, F32),
        pltpu.VMEM((NZ - 1,) + row, F32),
        pltpu.VMEM((NX, HEAD_CHUNKS) + chunk, BF16),
        pltpu.VMEM((NX - 1, HEAD_CHUNKS) + chunk, BF16),
        pltpu.VMEM((HEAD_CHUNKS,) + chunk, BF16),
        pltpu.VMEM((NZ - 1,) + chunk, BF16),
        pltpu.VMEM((NX, HEAD_CHUNKS) + chunk, BF16),
        pltpu.VMEM((NX, 2) + row, F32),
        pltpu.VMEM((NX - 1, 2) + row, F32),
        pltpu.VMEM((2,) + row, F32),
        pltpu.VMEM((NZ - 1, 2) + row, F32),
        pltpu.VMEM((NT, ROWS, 128), BF16),
        pltpu.VMEM((NX, FF_BLOCKS, 2) + chunk, BF16),
        pltpu.VMEM((NX - 1, FF_BLOCKS, 2) + chunk, BF16),
        pltpu.VMEM((FF_BLOCKS, 2) + chunk, BF16),
        pltpu.VMEM((NZ - 1, 2) + chunk, BF16),
        pltpu.VMEM((NX, FF_BLOCKS) + chunk, BF16),
        pltpu.VMEM(row, F32),
        pltpu.VMEM((NX - 1,) + row, F32),
        pltpu.VMEM(row, F32),
        pltpu.VMEM((NZ - 1,) + row, F32),
        pltpu.VMEM((NT, ROWS, 128), BF16),
        pltpu.SemaphoreType.DMA((17,)),
        pltpu.SemaphoreType.DMA((HEAD_CHUNKS,)),
        pltpu.SemaphoreType.DMA((HEAD_CHUNKS,)),
        pltpu.SemaphoreType.DMA((FF_BLOCKS,)),
        pltpu.SemaphoreType.DMA((9,)),
        pltpu.SemaphoreType.DMA((NT,)),
        pltpu.SemaphoreType.DMA((NT,)),
    ]
    result = pl.pallas_call(
        kernel,
        out_shape=jax.ShapeDtypeStruct(hidden_in.shape, BF16),
        in_specs=[pl.BlockSpec(memory_space=pltpu.SMEM)] + [vmem] * 3 + [anywhere] * 7,
        out_specs=vmem,
        scratch_shapes=scratch,
        compiler_params=pltpu.CompilerParams(
            collective_id=0, has_side_effects=True, vmem_limit_bytes=32 * 1024 * 1024
        ),
    )(
        block_lengths,
        hidden_in,
        attn_gain.reshape(1, -1),
        ffn_gain.reshape(1, -1),
        *weights,
    )
    present = jnp.arange(ROWS)[:, None] < question_length[0]
    return jnp.where(present, result, jnp.zeros_like(result))


def solution(mesh):
    placed = (
        P(None, "ctx"),
        P("ctx"),
        P("ctx", "tp"),
        P("ctx", "tp"),
        P("ctx", "tp"),
        P("ctx"),
        P(),
        P("tp", "ctx"),
        P("ctx"),
        P("ctx", "tp"),
        P("ctx", "tp"),
        P("tp", "ctx"),
    )
    return jax.shard_map(
        body, mesh=mesh, in_specs=placed, out_specs=P(None, "ctx"), check_vma=False
    )
```

```python
import functools
import math

import jax
import jax.numpy as jnp
from jax import lax
from jax.experimental import pallas as pl
from jax.experimental.pallas import tpu as pltpu
from jax.sharding import PartitionSpec as P

D = 8192
HD = 128
EPSILON = 1e-05
MASKED = -1e30
NX = 4
NZ = 16
NT = 8
ROWS = 64
CHUNKS = 8
FF_BLOCKS = 14
PIECES = 4
PIECE = NZ // PIECES
FAR_FIRST = (8, 7, 9, 6, 10, 5, 11, 4, 12, 3, 13, 2, 14, 1, 15)
NEAR = tuple(
    (dz % NZ, dx)
    for dz in (4, 3, -3, 2, -2, 1, -1, 0)
    for dx in (2, 1, 3, 0)
    if (dz, dx) != (0, 0)
)
NEAR_ONE_WAY = tuple((dz, dx) for dz, dx in NEAR if dz == 4 and dx != 0)
PARTNERS = NX - 1 + NZ - 1 + NT - 1 + 7 * 3 + 3
MESH = pl.DeviceIdType.MESH
F32 = jnp.float32
BF16 = jnp.bfloat16


def lane_row(column):
    shape = (column.shape[0], 128)
    same = lax.broadcasted_iota(jnp.int32, shape, 0) == lax.broadcasted_iota(jnp.int32, shape, 1)
    return jnp.sum(jnp.where(same, jnp.broadcast_to(column, shape), 0.0), axis=0, keepdims=True)


def row_column(row, base):
    shape = (16, 128)
    same = lax.broadcasted_iota(jnp.int32, shape, 0) + base == lax.broadcasted_iota(
        jnp.int32, shape, 1
    )
    return jnp.sum(jnp.where(same, jnp.broadcast_to(row, shape), 0.0), axis=1, keepdims=True)


def kernel(
    length_ref,
    hidden_hbm,
    attn_gain_hbm,
    ffn_gain_hbm,
    wq_hbm,
    key_hbm,
    value_hbm,
    wout_hbm,
    wgate_hbm,
    wup_hbm,
    wdown_hbm,
    out_ref,
    hidden,
    attn_gain,
    ffn_gain,
    wq,
    key,
    value,
    wout,
    wgate,
    wup,
    wdown,
    load_sems,
    send_sems,
    recv_sems,
    qx_src,
    qx_dst,
    qz_src,
    qz_dst,
    q_all,
    sx_src,
    sx_dst,
    sz_src,
    sz_dst,
    ax_src,
    ax_dst,
    az_src,
    az_dst,
    a_all,
    tx_src,
    tx_dst,
    tz_src,
    tz_dst,
    p_all,
    fx_src,
    fx_dst,
    fz_src,
    fz_dst,
    f_all,
    ux_src,
    ux_dst,
    uz_src,
    uz_dst,
    d_all,
    f_gather_sems,
    p_sems,
    d_sems,
):
    ctx = lax.axis_index("ctx")
    tp = lax.axis_index("tp")
    x = lax.rem(ctx, NX)
    z = lax.div(ctx, NX)

    def x_of(k):
        return lax.rem(x + k, NX)

    def z_of(k):
        return lax.rem(z + k, NZ)

    def t_of(k):
        return lax.rem(tp + k, NT)

    def device(dz, dx):
        return (z_of(dz) * NX + x_of(dx), tp)

    sources = (
        hidden_hbm,
        attn_gain_hbm,
        wq_hbm,
        key_hbm,
        value_hbm,
        ffn_gain_hbm,
        wout_hbm,
        wgate_hbm,
        wup_hbm,
        wdown_hbm,
    )
    targets = (hidden, attn_gain, wq, key, value, ffn_gain, wout, wgate, wup, wdown)
    loads = [
        pltpu.make_async_copy(source, target, load_sems.at[at])
        for at, (source, target) in enumerate(zip(sources, targets))
    ]
    for load in loads[:3]:
        load.start()

    barrier = pltpu.get_barrier_semaphore()

    def greet(peer):
        pl.semaphore_signal(barrier, inc=1, device_id=peer, device_id_type=MESH)

    for k in FAR_FIRST:
        greet(device(k, 0))
    for k in range(1, NX):
        greet(device(0, k))
    for k in range(1, NT):
        greet((ctx, t_of(k)))
    for dz, dx in NEAR:
        if dz != 0 and dx != 0:
            greet(device(dz, dx))
    for dz, dx in NEAR_ONE_WAY:
        greet(device(-dz % NZ, -dx % NX))
    for load in loads[3:]:
        load.start()

    def send(source, target, send_sem, recv_sem, peer):
        pltpu.make_async_remote_copy(
            src_ref=source,
            dst_ref=target,
            send_sem=send_sem,
            recv_sem=recv_sem,
            device_id=peer,
            device_id_type=MESH,
        ).start()

    def drain(ref, sem):
        pltpu.make_async_copy(ref, ref, sem).wait()

    pending = []

    def at_end(sem_at, ref, condition=None):
        pending.append((sem_at, ref, condition))

    def finish():
        for sem_at, ref, condition in pending:
            if condition is None:
                drain(ref, send_sems.at[sem_at])
            else:
                pl.when(condition)(functools.partial(drain, ref, send_sems.at[sem_at]))

    def x_scatter(source, target, at):
        for k in range(1, NX):
            send(source.at[x_of(k)], target.at[k - 1], send_sems.at[at], recv_sems.at[at], device(0, k))
        at_end(at, target)

    def x_same(source, target, at):
        for k in range(1, NX):
            send(source, target.at[k - 1], send_sems.at[at], recv_sems.at[at], device(0, k))
        at_end(at, target)

    def z_scatter(source, target, at, row_source, row_target, row_at):
        for k in FAR_FIRST:
            send(
                row_source,
                row_target.at[k - 1],
                send_sems.at[row_at],
                recv_sems.at[row_at],
                device(k, 0),
            )
            send(
                source.at[lax.rem(z + k, CHUNKS)],
                target.at[k - 1],
                send_sems.at[at],
                recv_sems.at[at],
                device(k, 0),
            )
        at_end(row_at, row_target)
        at_end(at, target)

    def near_gather(whole, at):
        own = x * CHUNKS + lax.rem(z, CHUNKS)
        for dz, dx in NEAR:
            send(whole.at[own], whole.at[own], send_sems.at[at], recv_sems.at[at], device(dz, dx))
        rest = whole.at[pl.ds(0, NX * CHUNKS - 1)]
        drain(rest, recv_sems.at[at])
        at_end(at, rest)

    loads[0].wait()
    loads[1].wait()
    stream = hidden[...].astype(F32)
    sx_src[...] = lane_row(jnp.sum(stream * stream, axis=1, keepdims=True))
    normed = (stream * attn_gain[...]).astype(BF16)
    loads[2].wait()
    query_part = jnp.dot(normed, wq[...], preferred_element_type=F32)
    for j in range(NX):
        for h in range(2):
            for g in range(4):
                column = (2 * j + h) * HD
                qx_src[j, 4 * h + g] = query_part[16 * g : 16 * g + 16, column : column + HD]
    pl.semaphore_wait(barrier, PARTNERS)

    x_same(sx_src, sx_dst, 0)
    x_scatter(qx_src, qx_dst, 1)
    drain(sx_dst, recv_sems.at[0])
    sz_src[...] = sx_src[...] + sx_dst[0] + sx_dst[1] + sx_dst[2]
    drain(qx_dst, recv_sems.at[1])
    qz_src[...] = qx_src[x] + qx_dst[0] + qx_dst[1] + qx_dst[2]
    z_scatter(qz_src, qz_dst, 3, sz_src, sz_dst, 2)
    mine = lax.rem(z, CHUNKS)
    slot = x * CHUNKS + mine
    drain(sz_dst, recv_sems.at[2])
    squares = jnp.sum(sz_dst[...], axis=0) + sz_src[...]
    scale = lax.rsqrt(row_column(squares, 16 * lax.rem(mine, 4)) / D + EPSILON)
    drain(qz_dst, recv_sems.at[3])
    total = qz_src[mine] + jnp.sum(qz_dst[...], axis=0)
    q_all[slot] = (scale * total).astype(BF16)
    near_gather(q_all, 4)

    loads[3].wait()
    loads[4].wait()
    queries = q_all[...].reshape(NX * CHUNKS * 16, HD)
    scores = lax.dot_general(
        key[...], queries, (((1,), (1,)), ((), ())), preferred_element_type=F32
    ) * (1.0 / math.sqrt(HD))
    usable = lax.broadcasted_iota(jnp.int32, scores.shape, 0) < length_ref[0]
    scores = jnp.where(usable, scores, MASKED)
    maxima = jnp.max(scores, axis=0, keepdims=True)
    weights = jnp.exp(scores - maxima)
    totals = jnp.sum(weights, axis=0, keepdims=True)
    for j in range(NX):
        tx_src[j, 0] = maxima[:, 128 * j : 128 * j + 128]
        tx_src[j, 1] = totals[:, 128 * j : 128 * j + 128]
    x_scatter(tx_src, tx_dst, 5)
    numerators = lax.dot_general(
        value[...], weights.astype(BF16), (((0,), (0,)), ((), ())), preferred_element_type=F32
    ).astype(BF16)
    for j in range(NX):
        for i in range(CHUNKS):
            ax_src[j, i] = numerators[16 * i : 16 * i + 16, 128 * j : 128 * j + 128]
    x_scatter(ax_src, ax_dst, 6)
    drain(tx_dst, recv_sems.at[5])
    pieces = [tx_src.at[x]] + [tx_dst.at[k] for k in range(NX - 1)]
    summit = pieces[0][0]
    for piece in pieces[1:]:
        summit = jnp.maximum(summit, piece[0])
    factors = [jnp.exp(piece[0] - summit) for piece in pieces]
    tz_src[0] = summit
    tz_src[1] = sum(factor * piece[1] for factor, piece in zip(factors, pieces))
    drain(ax_dst, recv_sems.at[6])
    merged = ax_src[x].astype(F32) * factors[0]
    for k in range(NX - 1):
        merged = merged + ax_dst[k].astype(F32) * factors[k + 1]
    az_src[...] = merged.astype(BF16)
    z_scatter(az_src, az_dst, 8, tz_src, tz_dst, 7)
    drain(tz_dst, recv_sems.at[7])
    own = tz_src[0]
    others = tz_dst[:, 0]
    summit = jnp.maximum(own, jnp.max(others, axis=0))
    own_factor = jnp.exp(own - summit)
    factors = jnp.exp(others - summit)
    total = own_factor * tz_src[1] + jnp.sum(factors * tz_dst[:, 1], axis=0)
    drain(az_dst, recv_sems.at[8])
    merged = own_factor * az_src[mine].astype(F32) + jnp.sum(
        factors * az_dst[...].astype(F32), axis=0
    )
    a_all[slot] = (merged / total).astype(BF16)
    near_gather(a_all, 9)

    loads[5].wait()
    loads[6].wait()
    turned = []
    for j in range(NX):
        block = a_all[CHUNKS * j : CHUNKS * j + CHUNKS].reshape(HD, 128).astype(F32)
        across = jnp.transpose(block).astype(BF16)
        turned += [across[:ROWS], across[ROWS:]]
    projected = jnp.dot(
        jnp.concatenate(turned, axis=1), wout[...], preferred_element_type=F32
    )

    def tp_sum(part, whole, at, sems):
        whole[tp] = part.astype(BF16)
        for k in (4, 5, 2, 3, 6, 7, 1):
            send(whole.at[tp], whole.at[tp], send_sems.at[at], sems.at[tp], (ctx, t_of(k)))
        for k in (1, 7, 6, 3, 2, 5, 4):
            source = t_of(k)
            drain(whole.at[source], sems.at[source])
        at_end(at, whole.at[pl.ds(0, NT - 1)])
        total = whole[0].astype(F32)
        for source in range(1, NT):
            total = total + whole[source].astype(F32)
        return total

    residual = hidden[...].astype(F32) + tp_sum(projected, p_all, 10, p_sems)

    ux_src[...] = lane_row(jnp.sum(residual * residual, axis=1, keepdims=True))
    x_same(ux_src, ux_dst, 11)
    second = (residual * ffn_gain[...]).astype(BF16)
    loads[7].wait()
    loads[8].wait()
    order = FAR_FIRST + (0,)
    for p in range(PIECES):
        for s in range(PIECE):
            block = jnp.minimum(z_of(order[p * PIECE + s]), FF_BLOCKS - 1)
            columns = pl.ds(pl.multiple_of(block * 128, 128), 128)
            pair = jnp.concatenate([wgate[:, columns], wup[:, columns]], axis=1)
            part = jnp.dot(second, pair, preferred_element_type=F32).astype(BF16)
            for j in range(NX):
                fx_src[p, j, s, 0] = part[16 * j : 16 * j + 16, :128]
                fx_src[p, j, s, 1] = part[16 * j : 16 * j + 16, 128:]
        x_scatter(fx_src.at[p], fx_dst.at[p], 12 + p)
    drain(ux_dst, recv_sems.at[11])
    uz_src[...] = ux_src[...] + ux_dst[0] + ux_dst[1] + ux_dst[2]
    for k in FAR_FIRST:
        send(uz_src, uz_dst.at[k - 1], send_sems.at[16], recv_sems.at[16], device(k, 0))
    at_end(16, uz_dst)
    for p in range(PIECES):
        drain(fx_dst.at[p], recv_sems.at[12 + p])
        fz_src[pl.ds(p * PIECE, PIECE)] = (
            fx_src[p, x].astype(F32)
            + fx_dst[p, 0].astype(F32)
            + fx_dst[p, 1].astype(F32)
            + fx_dst[p, 2].astype(F32)
        ).astype(BF16)
        for s in range(PIECE):
            k = order[p * PIECE + s]
            if k == 0:
                continue

            @pl.when(z_of(k) < FF_BLOCKS)
            def _():
                send(
                    fz_src.at[p * PIECE + s],
                    fz_dst.at[k - 1],
                    send_sems.at[17],
                    recv_sems.at[17],
                    device(k, 0),
                )

    reduces = z < FF_BLOCKS
    at_end(17, fz_dst.at[pl.ds(0, FF_BLOCKS - 1)], reduces)
    at_end(17, fz_dst.at[pl.ds(0, FF_BLOCKS)], jnp.logical_not(reduces))
    drain(uz_dst, recv_sems.at[16])
    squares = jnp.sum(uz_dst[...], axis=0) + uz_src[...]
    scale = lax.rsqrt(row_column(squares, 16 * x) / D + EPSILON)

    def x_forward(block):
        for k in (2, 1, 3):
            send(
                f_all.at[x, block],
                f_all.at[x, block],
                send_sems.at[19],
                recv_sems.at[19],
                device(0, k),
            )

    @pl.when(reduces)
    def _():
        drain(fz_dst, recv_sems.at[17])
        both = fz_src[NZ - 1].astype(F32) + jnp.sum(fz_dst[...].astype(F32), axis=0)
        gate = scale * both[0]
        up = scale * both[1]
        f_all[x, z] = (gate / (1.0 + jnp.exp(-gate)) * up).astype(BF16)
        for k in FAR_FIRST:
            send(f_all.at[x, z], f_all.at[x, z], send_sems.at[18], f_gather_sems.at[z], device(k, 0))
        x_forward(z)

    at_end(18, az_dst, reduces)

    for k in reversed(FAR_FIRST):
        block = z_of(k)

        @pl.when(block < FF_BLOCKS)
        def _():
            drain(f_all.at[x, block], f_gather_sems.at[block])
            x_forward(block)

    drain(f_all.at[pl.ds(0, NX - 1)], recv_sems.at[19])
    at_end(19, f_all.at[pl.ds(0, NX - 1)])

    loads[9].wait()
    activated = jnp.concatenate(
        [f_all[:, b].reshape(ROWS, 128) for b in range(FF_BLOCKS)], axis=1
    )
    lowered = jnp.dot(activated, wdown[...], preferred_element_type=F32)
    result = residual + tp_sum(lowered, d_all, 20, d_sems)
    out_ref[...] = result.astype(BF16)
    finish()


def body(
    hidden_in,
    attn_gain,
    w_query,
    key_cache,
    value_cache,
    block_lengths,
    question_length,
    w_out,
    ffn_gain,
    w_gate,
    w_up,
    w_down,
):
    operands = (
        hidden_in,
        attn_gain.reshape(1, -1),
        ffn_gain.reshape(1, -1),
        w_query,
        key_cache,
        value_cache,
        w_out,
        w_gate,
        w_up,
        w_down,
    )
    chunk = (16, 128)
    row = (1, 128)
    dma = pltpu.SemaphoreType.DMA
    scratch = [pltpu.VMEM(a.shape, a.dtype) for a in operands]
    scratch += [dma((len(operands),)), dma((21,)), dma((21,))]
    scratch += [
        pltpu.VMEM((NX, CHUNKS) + chunk, F32),
        pltpu.VMEM((NX - 1, CHUNKS) + chunk, F32),
        pltpu.VMEM((CHUNKS,) + chunk, F32),
        pltpu.VMEM((NZ - 1,) + chunk, F32),
        pltpu.VMEM((NX * CHUNKS,) + chunk, BF16),
        pltpu.VMEM(row, F32),
        pltpu.VMEM((NX - 1,) + row, F32),
        pltpu.VMEM(row, F32),
        pltpu.VMEM((NZ - 1,) + row, F32),
        pltpu.VMEM((NX, CHUNKS) + chunk, BF16),
        pltpu.VMEM((NX - 1, CHUNKS) + chunk, BF16),
        pltpu.VMEM((CHUNKS,) + chunk, BF16),
        pltpu.VMEM((NZ - 1,) + chunk, BF16),
        pltpu.VMEM((NX * CHUNKS,) + chunk, BF16),
        pltpu.VMEM((NX, 2) + row, F32),
        pltpu.VMEM((NX - 1, 2) + row, F32),
        pltpu.VMEM((2,) + row, F32),
        pltpu.VMEM((NZ - 1, 2) + row, F32),
        pltpu.VMEM((NT, ROWS, 128), BF16),
        pltpu.VMEM((PIECES, NX, PIECE, 2) + chunk, BF16),
        pltpu.VMEM((PIECES, NX - 1, PIECE, 2) + chunk, BF16),
        pltpu.VMEM((NZ, 2) + chunk, BF16),
        pltpu.VMEM((NZ - 1, 2) + chunk, BF16),
        pltpu.VMEM((NX, FF_BLOCKS) + chunk, BF16),
        pltpu.VMEM(row, F32),
        pltpu.VMEM((NX - 1,) + row, F32),
        pltpu.VMEM(row, F32),
        pltpu.VMEM((NZ - 1,) + row, F32),
        pltpu.VMEM((NT, ROWS, 128), BF16),
        dma((FF_BLOCKS,)),
        dma((NT,)),
        dma((NT,)),
    ]
    result = pl.pallas_call(
        kernel,
        out_shape=jax.ShapeDtypeStruct(hidden_in.shape, BF16),
        in_specs=[pl.BlockSpec(memory_space=pltpu.SMEM)]
        + [pl.BlockSpec(memory_space=pl.ANY)] * len(operands),
        out_specs=pl.BlockSpec(memory_space=pltpu.VMEM),
        scratch_shapes=scratch,
        compiler_params=pltpu.CompilerParams(
            collective_id=0, has_side_effects=True, vmem_limit_bytes=60 * 1024 * 1024
        ),
    )(block_lengths, *operands)
    present = jnp.arange(ROWS)[:, None] < question_length[0]
    return jnp.where(present, result, jnp.zeros_like(result))


def solution(mesh):
    placed = (
        P(None, "ctx"),
        P("ctx"),
        P("ctx", "tp"),
        P("ctx", "tp"),
        P("ctx", "tp"),
        P("ctx"),
        P(),
        P("tp", "ctx"),
        P("ctx"),
        P("ctx", "tp"),
        P("ctx", "tp"),
        P("tp", "ctx"),
    )
    return jax.shard_map(
        body, mesh=mesh, in_specs=placed, out_specs=P(None, "ctx"), check_vma=False
    )
```

```python
import functools
import math

import jax
import jax.numpy as jnp
from jax import lax
from jax.experimental import pallas as pl
from jax.experimental.pallas import tpu as pltpu
from jax.sharding import PartitionSpec as P

D = 8192
HD = 128
EPSILON = 1e-05
MASKED = -1e30
NX = 4
NZ = 16
NT = 8
ROWS = 64
BLOCK = 512
CHUNKS = 8
FF_BLOCKS = 14
PIECES = 4
PIECE = NZ // PIECES
FAR_FIRST = (8, 7, 9, 6, 10, 5, 11, 4, 12, 3, 13, 2, 14, 1, 15)
QUERY_OFFSETS = ((8, 7, 9, 6, 14, 1, 15), (10, 5, 11, 4, 12, 3, 13, 2))
NEAR_Z = (4, 3, 13, 2, 14, 1, 15)
NEAR = tuple(
    (dz % NZ, dx)
    for dz in (4, 3, -3, 2, -2, 1, -1, 0)
    for dx in (2, 1, 3, 0)
    if (dz, dx) != (0, 0)
)
MESH = pl.DeviceIdType.MESH
F32 = jnp.float32
BF16 = jnp.bfloat16


def lane_row(column):
    shape = (column.shape[0], 128)
    same = lax.broadcasted_iota(jnp.int32, shape, 0) == lax.broadcasted_iota(jnp.int32, shape, 1)
    return jnp.sum(jnp.where(same, jnp.broadcast_to(column, shape), 0.0), axis=0, keepdims=True)


def row_column(row, base):
    shape = (16, 128)
    same = lax.broadcasted_iota(jnp.int32, shape, 0) + base == lax.broadcasted_iota(
        jnp.int32, shape, 1
    )
    return jnp.sum(jnp.where(same, jnp.broadcast_to(row, shape), 0.0), axis=1, keepdims=True)


def kernel(
    length_ref,
    hidden_hbm,
    attn_gain_hbm,
    ffn_gain_hbm,
    wq_hbm,
    key_hbm,
    value_hbm,
    wout_hbm,
    wgate_hbm,
    wup_hbm,
    wdown_hbm,
    out_ref,
    hidden,
    attn_gain,
    ffn_gain,
    wq,
    key,
    value,
    wout,
    wgate,
    wup,
    wdown,
    load_sems,
    send_sems,
    recv_sems,
    qx_src,
    qx_dst,
    qz_src,
    qz_dst,
    q_all,
    sx_src,
    sx_dst,
    sz_src,
    sz_dst,
    kx_dst,
    vx_dst,
    lx_src,
    lx_dst,
    v_turned,
    w_turned,
    az_src,
    az_dst,
    a_all,
    tz_src,
    tz_dst,
    p_all,
    fx_src,
    fx_dst,
    fz_src,
    fz_dst,
    f_all,
    ux_src,
    ux_dst,
    uz_src,
    uz_dst,
    d_all,
    word_sems,
    f_gather_sems,
    p_sems,
    d_sems,
):
    ctx = lax.axis_index("ctx")
    tp = lax.axis_index("tp")
    x = lax.rem(ctx, NX)
    z = lax.div(ctx, NX)

    def x_of(k):
        return lax.rem(x + k, NX)

    def z_of(k):
        return lax.rem(z + k, NZ)

    def t_of(k):
        return lax.rem(tp + k, NT)

    def device(dz, dx):
        return (z_of(dz) * NX + x_of(dx), tp)

    sources = (
        hidden_hbm,
        attn_gain_hbm,
        wq_hbm,
        key_hbm,
        value_hbm,
        ffn_gain_hbm,
        wout_hbm,
        wgate_hbm,
        wup_hbm,
        wdown_hbm,
    )
    targets = (hidden, attn_gain, wq, key, value, ffn_gain, wout, wgate, wup, wdown)
    loads = [
        pltpu.make_async_copy(source, target, load_sems.at[at])
        for at, (source, target) in enumerate(zip(sources, targets))
    ]
    for load in loads[:3]:
        load.start()

    barrier = pltpu.get_barrier_semaphore()
    for k in (2, 14, 1, 15):
        pl.semaphore_signal(barrier, inc=1, device_id=device(k, 0), device_id_type=MESH)
    for k in range(1, NX):
        pl.semaphore_signal(barrier, inc=1, device_id=device(0, k), device_id_type=MESH)
    for k in range(1, NT):
        pl.semaphore_signal(barrier, inc=1, device_id=(ctx, t_of(k)), device_id_type=MESH)

    def pass_on(step):
        for k in (step, NZ - step):
            pl.semaphore_signal(
                word_sems.at[step // 4], inc=1, device_id=device(k, 0), device_id_type=MESH
            )

    def word(step):
        pl.semaphore_wait(word_sems.at[step // 4], 2)

    for load in loads[3:]:
        load.start()

    def send(source, target, send_sem, recv_sem, peer):
        pltpu.make_async_remote_copy(
            src_ref=source,
            dst_ref=target,
            send_sem=send_sem,
            recv_sem=recv_sem,
            device_id=peer,
            device_id_type=MESH,
        ).start()

    def drain(ref, sem):
        pltpu.make_async_copy(ref, ref, sem).wait()

    pending = []

    def at_end(sem_at, ref, condition=None):
        pending.append((sem_at, ref, condition))

    def finish():
        for sem_at, ref, condition in pending:
            if condition is None:
                drain(ref, send_sems.at[sem_at])
            else:
                pl.when(condition)(functools.partial(drain, ref, send_sems.at[sem_at]))

    def x_scatter(source, target, at):
        for k in range(1, NX):
            send(source.at[x_of(k)], target.at[k - 1], send_sems.at[at], recv_sems.at[at], device(0, k))
        at_end(at, target)

    def x_same(source, target, at):
        for k in range(1, NX):
            send(source, target.at[k - 1], send_sems.at[at], recv_sems.at[at], device(0, k))
        at_end(at, target)

    def z_scatter(source, target, at, row_source, row_target, row_at):
        for k in FAR_FIRST:
            send(
                row_source,
                row_target.at[k - 1],
                send_sems.at[row_at],
                recv_sems.at[row_at],
                device(k, 0),
            )
            send(
                source.at[lax.rem(z + k, CHUNKS)],
                target.at[k - 1],
                send_sems.at[at],
                recv_sems.at[at],
                device(k, 0),
            )
        at_end(row_at, row_target)
        at_end(at, target)

    def near_gather(whole, at):
        own = x * CHUNKS + lax.rem(z, CHUNKS)
        for dz, dx in NEAR:
            send(whole.at[own], whole.at[own], send_sems.at[at], recv_sems.at[at], device(dz, dx))
        rest = whole.at[pl.ds(0, NX * CHUNKS - 1)]
        drain(rest, recv_sems.at[at])
        at_end(at, rest)

    loads[0].wait()
    loads[1].wait()
    stream = hidden[...].astype(F32)
    sx_src[...] = lane_row(jnp.sum(stream * stream, axis=1, keepdims=True))
    normed = (stream * attn_gain[...]).astype(BF16)
    loads[2].wait()
    query_part = jnp.dot(normed, wq[...], preferred_element_type=F32)
    for i in range(CHUNKS):
        place = lax.rem(i - z + NZ + 2, CHUNKS)
        for j in range(NX):
            column = (2 * j + i // 4) * HD
            row = 16 * (i % 4)
            qx_src[lax.div(place, 4), j, lax.rem(place, 4)] = query_part[
                row : row + 16, column : column + HD
            ]
    pl.semaphore_wait(barrier, 4 + NX - 1 + NT - 1)
    pass_on(2)

    x_same(sx_src, sx_dst, 0)
    for p in range(2):
        x_scatter(qx_src.at[p], qx_dst.at[p], 1 + p)
    word(2)
    pass_on(4)
    loads[3].wait()
    loads[4].wait()
    lx_src[...] = jnp.full((1, 128), length_ref[0].astype(F32), F32)
    drain(sx_dst, recv_sems.at[0])
    sz_src[...] = sx_src[...] + sx_dst[0] + sx_dst[1] + sx_dst[2]
    word(4)
    for p, offsets in enumerate(QUERY_OFFSETS):
        drain(qx_dst.at[p], recv_sems.at[1 + p])
        qz_src[pl.ds(4 * p, 4)] = qx_src[p, x] + qx_dst[p, 0] + qx_dst[p, 1] + qx_dst[p, 2]
        for k in offsets:
            send(sz_src, sz_dst.at[k - 1], send_sems.at[3], recv_sems.at[3], device(k, 0))
            send(
                qz_src.at[(k + 2) % CHUNKS],
                qz_dst.at[k - 1],
                send_sems.at[4],
                recv_sems.at[4],
                device(k, 0),
            )
    at_end(3, sz_dst)
    at_end(4, qz_dst)
    x_same(lx_src, lx_dst, 5)
    x_same(key, kx_dst, 6)
    x_same(value, vx_dst, 7)
    mine = lax.rem(z, CHUNKS)
    slot = x * CHUNKS + mine
    drain(sz_dst, recv_sems.at[3])
    squares = jnp.sum(sz_dst[...], axis=0) + sz_src[...]
    scale = lax.rsqrt(row_column(squares, 16 * lax.rem(mine, 4)) / D + EPSILON)
    drain(qz_dst, recv_sems.at[4])
    total = qz_src[2] + jnp.sum(qz_dst[...], axis=0)
    q_all[mine] = (scale * total).astype(BF16)
    for dz in NEAR_Z:
        send(q_all.at[mine], q_all.at[mine], send_sems.at[8], recv_sems.at[8], device(dz, 0))
    at_end(8, q_all.at[pl.ds(0, CHUNKS - 1)])
    loads[6].wait()
    for j in range(NX):
        for h in range(2):
            at = (2 * j + h) * HD
            w_turned[pl.ds(HD * h, HD), pl.ds(HD * j, HD)] = jnp.transpose(
                wout[at : at + HD].astype(F32)
            ).astype(BF16)
    drain(lx_dst, recv_sems.at[5])
    drain(kx_dst, recv_sems.at[6])
    drain(vx_dst, recv_sems.at[7])
    keys = [key] + [kx_dst.at[k] for k in range(NX - 1)]
    values = [value] + [vx_dst.at[k] for k in range(NX - 1)]
    lengths = [lx_src] + [lx_dst.at[k] for k in range(NX - 1)]
    for n in range(NX):
        v_turned[n] = jnp.transpose(values[n][...].astype(F32)).astype(BF16)
    drain(q_all.at[pl.ds(0, CHUNKS - 1)], recv_sems.at[8])

    queries = q_all[...].reshape(CHUNKS * 16, HD)
    token = lax.broadcasted_iota(jnp.int32, (BLOCK, 128), 0).astype(F32)
    found = []
    for n in range(NX):
        scores = lax.dot_general(
            keys[n][...], queries, (((1,), (1,)), ((), ())), preferred_element_type=F32
        ) * (1.0 / math.sqrt(HD))
        scores = jnp.where(token < lengths[n][...], scores, MASKED)
        maxima = jnp.max(scores, axis=0, keepdims=True)
        weights = jnp.exp(scores - maxima)
        totals = jnp.sum(weights, axis=0, keepdims=True)
        numerators = jnp.dot(v_turned[n], weights.astype(BF16), preferred_element_type=F32)
        found.append((maxima, totals, numerators))
    summit = functools.reduce(jnp.maximum, [piece[0] for piece in found])
    factors = [jnp.exp(piece[0] - summit) for piece in found]
    tz_src[0] = summit
    tz_src[1] = sum(factor * piece[1] for factor, piece in zip(factors, found))
    merged = sum(factor * piece[2] for factor, piece in zip(factors, found))
    for i in range(CHUNKS):
        az_src[i] = merged[16 * i : 16 * i + 16].astype(BF16)
    z_scatter(az_src, az_dst, 10, tz_src, tz_dst, 9)
    drain(tz_dst, recv_sems.at[9])
    own = tz_src[0]
    others = tz_dst[:, 0]
    summit = jnp.maximum(own, jnp.max(others, axis=0))
    own_factor = jnp.exp(own - summit)
    factors = jnp.exp(others - summit)
    total = own_factor * tz_src[1] + jnp.sum(factors * tz_dst[:, 1], axis=0)
    drain(az_dst, recv_sems.at[10])
    merged = own_factor * az_src[mine].astype(F32) + jnp.sum(
        factors * az_dst[...].astype(F32), axis=0
    )
    a_all[slot] = (merged / total).astype(BF16)
    near_gather(a_all, 11)

    both = jnp.dot(
        w_turned[...], a_all[...].reshape(NX * HD, 128), preferred_element_type=F32
    )
    projected = jnp.transpose(both[:HD, :ROWS] + both[HD:, ROWS:])

    def tp_sum(part, whole, at, sems):
        whole[tp] = part.astype(BF16)
        for k in (4, 5, 2, 3, 6, 7, 1):
            send(whole.at[tp], whole.at[tp], send_sems.at[at], sems.at[tp], (ctx, t_of(k)))
        for k in (1, 7, 6, 3, 2, 5, 4):
            source = t_of(k)
            drain(whole.at[source], sems.at[source])
        at_end(at, whole.at[pl.ds(0, NT - 1)])
        total = whole[0].astype(F32)
        for source in range(1, NT):
            total = total + whole[source].astype(F32)
        return total

    residual = hidden[...].astype(F32) + tp_sum(projected, p_all, 12, p_sems)

    loads[5].wait()
    ux_src[...] = lane_row(jnp.sum(residual * residual, axis=1, keepdims=True))
    x_same(ux_src, ux_dst, 13)
    second = (residual * ffn_gain[...]).astype(BF16)
    loads[7].wait()
    loads[8].wait()
    order = FAR_FIRST + (0,)
    for p in range(PIECES):
        for s in range(PIECE):
            block = jnp.minimum(z_of(order[p * PIECE + s]), FF_BLOCKS - 1)
            columns = pl.ds(pl.multiple_of(block * 128, 128), 128)
            pair = jnp.concatenate([wgate[:, columns], wup[:, columns]], axis=1)
            part = jnp.dot(second, pair, preferred_element_type=F32).astype(BF16)
            for j in range(NX):
                fx_src[p, j, s, 0] = part[16 * j : 16 * j + 16, :128]
                fx_src[p, j, s, 1] = part[16 * j : 16 * j + 16, 128:]
        x_scatter(fx_src.at[p], fx_dst.at[p], 14 + p)
    drain(ux_dst, recv_sems.at[13])
    uz_src[...] = ux_src[...] + ux_dst[0] + ux_dst[1] + ux_dst[2]
    for k in FAR_FIRST:
        send(uz_src, uz_dst.at[k - 1], send_sems.at[18], recv_sems.at[18], device(k, 0))
    at_end(18, uz_dst)
    for p in range(PIECES):
        drain(fx_dst.at[p], recv_sems.at[14 + p])
        fz_src[pl.ds(p * PIECE, PIECE)] = (
            fx_src[p, x].astype(F32)
            + fx_dst[p, 0].astype(F32)
            + fx_dst[p, 1].astype(F32)
            + fx_dst[p, 2].astype(F32)
        ).astype(BF16)
        for s in range(PIECE):
            k = order[p * PIECE + s]
            if k == 0:
                continue

            @pl.when(z_of(k) < FF_BLOCKS)
            def _():
                send(
                    fz_src.at[p * PIECE + s],
                    fz_dst.at[k - 1],
                    send_sems.at[19],
                    recv_sems.at[19],
                    device(k, 0),
                )

    reduces = z < FF_BLOCKS
    at_end(19, fz_dst.at[pl.ds(0, FF_BLOCKS - 1)], reduces)
    at_end(19, fz_dst.at[pl.ds(0, FF_BLOCKS)], jnp.logical_not(reduces))
    drain(uz_dst, recv_sems.at[18])
    squares = jnp.sum(uz_dst[...], axis=0) + uz_src[...]
    scale = lax.rsqrt(row_column(squares, 16 * x) / D + EPSILON)

    def x_forward(block):
        for k in (2, 1, 3):
            send(
                f_all.at[x, block],
                f_all.at[x, block],
                send_sems.at[21],
                recv_sems.at[21],
                device(0, k),
            )

    @pl.when(reduces)
    def _():
        drain(fz_dst, recv_sems.at[19])
        both = fz_src[NZ - 1].astype(F32) + jnp.sum(fz_dst[...].astype(F32), axis=0)
        gate = scale * both[0]
        up = scale * both[1]
        f_all[x, z] = (gate / (1.0 + jnp.exp(-gate)) * up).astype(BF16)
        for k in FAR_FIRST:
            send(f_all.at[x, z], f_all.at[x, z], send_sems.at[20], f_gather_sems.at[z], device(k, 0))
        x_forward(z)

    at_end(20, az_dst, reduces)

    for k in reversed(FAR_FIRST):
        block = z_of(k)

        @pl.when(block < FF_BLOCKS)
        def _():
            drain(f_all.at[x, block], f_gather_sems.at[block])
            x_forward(block)

    drain(f_all.at[pl.ds(0, NX - 1)], recv_sems.at[21])
    at_end(21, f_all.at[pl.ds(0, NX - 1)])

    loads[9].wait()
    activated = jnp.concatenate(
        [f_all[:, b].reshape(ROWS, 128) for b in range(FF_BLOCKS)], axis=1
    )
    lowered = jnp.dot(activated, wdown[...], preferred_element_type=F32)
    result = residual + tp_sum(lowered, d_all, 22, d_sems)
    out_ref[...] = result.astype(BF16)
    finish()


def body(
    hidden_in,
    attn_gain,
    w_query,
    key_cache,
    value_cache,
    block_lengths,
    question_length,
    w_out,
    ffn_gain,
    w_gate,
    w_up,
    w_down,
):
    operands = (
        hidden_in,
        attn_gain.reshape(1, -1),
        ffn_gain.reshape(1, -1),
        w_query,
        key_cache,
        value_cache,
        w_out,
        w_gate,
        w_up,
        w_down,
    )
    chunk = (16, 128)
    row = (1, 128)
    dma = pltpu.SemaphoreType.DMA
    scratch = [pltpu.VMEM(a.shape, a.dtype) for a in operands]
    scratch += [dma((len(operands),)), dma((23,)), dma((23,))]
    scratch += [
        pltpu.VMEM((2, NX, 4) + chunk, F32),
        pltpu.VMEM((2, NX - 1, 4) + chunk, F32),
        pltpu.VMEM((CHUNKS,) + chunk, F32),
        pltpu.VMEM((NZ - 1,) + chunk, F32),
        pltpu.VMEM((CHUNKS,) + chunk, BF16),
        pltpu.VMEM(row, F32),
        pltpu.VMEM((NX - 1,) + row, F32),
        pltpu.VMEM(row, F32),
        pltpu.VMEM((NZ - 1,) + row, F32),
        pltpu.VMEM((NX - 1, BLOCK, HD), BF16),
        pltpu.VMEM((NX - 1, BLOCK, HD), BF16),
        pltpu.VMEM(row, F32),
        pltpu.VMEM((NX - 1,) + row, F32),
        pltpu.VMEM((NX, HD, BLOCK), BF16),
        pltpu.VMEM((2 * HD, NX * HD), BF16),
        pltpu.VMEM((CHUNKS,) + chunk, BF16),
        pltpu.VMEM((NZ - 1,) + chunk, BF16),
        pltpu.VMEM((NX * CHUNKS,) + chunk, BF16),
        pltpu.VMEM((2,) + row, F32),
        pltpu.VMEM((NZ - 1, 2) + row, F32),
        pltpu.VMEM((NT, ROWS, 128), BF16),
        pltpu.VMEM((PIECES, NX, PIECE, 2) + chunk, BF16),
        pltpu.VMEM((PIECES, NX - 1, PIECE, 2) + chunk, BF16),
        pltpu.VMEM((NZ, 2) + chunk, BF16),
        pltpu.VMEM((NZ - 1, 2) + chunk, BF16),
        pltpu.VMEM((NX, FF_BLOCKS) + chunk, BF16),
        pltpu.VMEM(row, F32),
        pltpu.VMEM((NX - 1,) + row, F32),
        pltpu.VMEM(row, F32),
        pltpu.VMEM((NZ - 1,) + row, F32),
        pltpu.VMEM((NT, ROWS, 128), BF16),
        pltpu.SemaphoreType.REGULAR((2,)),
        dma((FF_BLOCKS,)),
        dma((NT,)),
        dma((NT,)),
    ]
    result = pl.pallas_call(
        kernel,
        out_shape=jax.ShapeDtypeStruct(hidden_in.shape, BF16),
        in_specs=[pl.BlockSpec(memory_space=pltpu.SMEM)]
        + [pl.BlockSpec(memory_space=pl.ANY)] * len(operands),
        out_specs=pl.BlockSpec(memory_space=pltpu.VMEM),
        scratch_shapes=scratch,
        compiler_params=pltpu.CompilerParams(
            collective_id=0, has_side_effects=True, vmem_limit_bytes=60 * 1024 * 1024
        ),
    )(block_lengths, *operands)
    present = jnp.arange(ROWS)[:, None] < question_length[0]
    return jnp.where(present, result, jnp.zeros_like(result))


def solution(mesh):
    placed = (
        P(None, "ctx"),
        P("ctx"),
        P("ctx", "tp"),
        P("ctx", "tp"),
        P("ctx", "tp"),
        P("ctx"),
        P(),
        P("tp", "ctx"),
        P("ctx"),
        P("ctx", "tp"),
        P("ctx", "tp"),
        P("tp", "ctx"),
    )
    return jax.shard_map(
        body, mesh=mesh, in_specs=placed, out_specs=P(None, "ctx"), check_vma=False
    )
```

```python
import functools
import math

import jax
import jax.numpy as jnp
from jax import lax
from jax.experimental import pallas as pl
from jax.experimental.pallas import tpu as pltpu
from jax.sharding import PartitionSpec as P

D = 8192
HD = 128
EPSILON = 1e-05
MASKED = -1e30
LAST = 22
NX = 4
NZ = 16
NT = 8
ROWS = 64
BLOCK = 512
CHUNKS = 8
FF_BLOCKS = 14
PIECES = ((0, 2), (2, 3), (5, 5), (10, 6))
FAR_FIRST = (8, 7, 9, 6, 10, 5, 11, 4, 12, 3, 13, 2, 14, 1, 15)
QUERY_OFFSETS = ((8, 7, 9, 6, 14, 1, 15), (10, 5, 11, 4, 12, 3, 13, 2))
NEAR_Z = (4, 3, 13, 2, 14, 1, 15)
NEAR = tuple(
    (dz % NZ, dx)
    for dz in (4, 3, -3, 2, -2, 1, -1, 0)
    for dx in (2, 1, 3, 0)
    if (dz, dx) != (0, 0)
)
MESH = pl.DeviceIdType.MESH
F32 = jnp.float32
BF16 = jnp.bfloat16


def lane_row(column):
    shape = (column.shape[0], 128)
    same = lax.broadcasted_iota(jnp.int32, shape, 0) == lax.broadcasted_iota(jnp.int32, shape, 1)
    return jnp.sum(jnp.where(same, jnp.broadcast_to(column, shape), 0.0), axis=0, keepdims=True)


def row_column(row, base):
    shape = (16, 128)
    same = lax.broadcasted_iota(jnp.int32, shape, 0) + base == lax.broadcasted_iota(
        jnp.int32, shape, 1
    )
    return jnp.sum(jnp.where(same, jnp.broadcast_to(row, shape), 0.0), axis=1, keepdims=True)


def kernel(
    length_ref,
    hidden_hbm,
    attn_gain_hbm,
    ffn_gain_hbm,
    wq_hbm,
    key_hbm,
    value_hbm,
    wout_hbm,
    wgate_hbm,
    wup_hbm,
    wdown_hbm,
    out_ref,
    hidden,
    attn_gain,
    ffn_gain,
    wq,
    key,
    value,
    wout,
    wgate,
    wup,
    wdown,
    load_sems,
    send_sems,
    recv_sems,
    qx_src,
    qx_dst,
    qz_src,
    qz_dst,
    q_all,
    sx_src,
    sx_dst,
    sz_src,
    sz_dst,
    kx_dst,
    vx_dst,
    lx_src,
    lx_dst,
    v_turned,
    w_turned,
    az_src,
    az_dst,
    a_all,
    tz_src,
    tz_dst,
    p_all,
    fx_src,
    fx_dst,
    fz_src,
    fz_dst,
    f_all,
    ux_src,
    ux_dst,
    uz_src,
    uz_dst,
    d_all,
    word_sems,
    f_gather_sems,
    p_sems,
    d_sems,
):
    ctx = lax.axis_index("ctx")
    tp = lax.axis_index("tp")
    x = lax.rem(ctx, NX)
    z = lax.div(ctx, NX)

    def x_of(k):
        return lax.rem(x + k, NX)

    def z_of(k):
        return lax.rem(z + k, NZ)

    def t_of(k):
        return lax.rem(tp + k, NT)

    def device(dz, dx):
        return (z_of(dz) * NX + x_of(dx), tp)

    sources = (
        hidden_hbm,
        attn_gain_hbm,
        wq_hbm,
        key_hbm,
        value_hbm,
        ffn_gain_hbm,
        wout_hbm,
        wgate_hbm,
        wup_hbm,
        wdown_hbm,
    )
    targets = (hidden, attn_gain, wq, key, value, ffn_gain, wout, wgate, wup, wdown)
    loads = [
        pltpu.make_async_copy(source, target, load_sems.at[at])
        for at, (source, target) in enumerate(zip(sources, targets))
    ]
    barrier = pltpu.get_barrier_semaphore()
    for k in (2, 14, 1, 15):
        pl.semaphore_signal(barrier, inc=1, device_id=device(k, 0), device_id_type=MESH)
    for k in range(1, NX):
        pl.semaphore_signal(barrier, inc=1, device_id=device(0, k), device_id_type=MESH)
    for k in range(1, NT):
        pl.semaphore_signal(barrier, inc=1, device_id=(ctx, t_of(k)), device_id_type=MESH)

    for load in loads:
        load.start()

    def pass_on(step):
        for k in (step, NZ - step):
            pl.semaphore_signal(
                word_sems.at[step // 4], inc=1, device_id=device(k, 0), device_id_type=MESH
            )

    def word(step):
        pl.semaphore_wait(word_sems.at[step // 4], 2)

    def send(source, target, send_sem, recv_sem, peer):
        pltpu.make_async_remote_copy(
            src_ref=source,
            dst_ref=target,
            send_sem=send_sem,
            recv_sem=recv_sem,
            device_id=peer,
            device_id_type=MESH,
        ).start()

    def drain(ref, sem):
        pltpu.make_async_copy(ref, ref, sem).wait()

    pending = []

    def at_end(sem_at, ref, condition=None):
        pending.append((sem_at, ref, condition))

    def finish():
        for sem_at, ref, condition in pending:
            if condition is None:
                drain(ref, send_sems.at[sem_at])
            else:
                pl.when(condition)(functools.partial(drain, ref, send_sems.at[sem_at]))

    def x_scatter(source, target, at):
        for k in range(1, NX):
            send(source.at[x_of(k)], target.at[k - 1], send_sems.at[at], recv_sems.at[at], device(0, k))
        at_end(at, target)

    def x_same(source, target, at):
        for k in range(1, NX):
            send(source, target.at[k - 1], send_sems.at[at], recv_sems.at[at], device(0, k))
        at_end(at, target)

    def z_scatter(source, target, at, row_source, row_target, row_at):
        for k in FAR_FIRST:
            send(
                row_source,
                row_target.at[k - 1],
                send_sems.at[row_at],
                recv_sems.at[row_at],
                device(k, 0),
            )
            send(
                source.at[lax.rem(z + k, CHUNKS)],
                target.at[k - 1],
                send_sems.at[at],
                recv_sems.at[at],
                device(k, 0),
            )
        at_end(row_at, row_target)
        at_end(at, target)

    def near_gather(whole, at):
        own = x * CHUNKS + lax.rem(z, CHUNKS)
        for dz, dx in NEAR:
            send(whole.at[own], whole.at[own], send_sems.at[at], recv_sems.at[at], device(dz, dx))
        rest = whole.at[pl.ds(0, NX * CHUNKS - 1)]
        drain(rest, recv_sems.at[at])
        at_end(at, rest)

    loads[0].wait()
    loads[1].wait()
    stream = hidden[...].astype(F32)
    normed = (stream * attn_gain[...]).astype(BF16)
    loads[2].wait()
    query_part = jnp.dot(normed, wq[...], preferred_element_type=F32)
    for i in range(CHUNKS):
        place = lax.rem(i - z + NZ + 2, CHUNKS)
        for j in range(NX):
            column = (2 * j + i // 4) * HD
            row = 16 * (i % 4)
            qx_src[lax.div(place, 4), j, lax.rem(place, 4)] = query_part[
                row : row + 16, column : column + HD
            ]
    pl.semaphore_wait(barrier, 4 + NX - 1 + NT - 1)
    pass_on(2)

    for p in range(2):
        x_scatter(qx_src.at[p], qx_dst.at[p], 1 + p)
    sx_src[...] = lane_row(jnp.sum(stream * stream, axis=1, keepdims=True))
    x_same(sx_src, sx_dst, 0)
    word(2)
    pass_on(4)
    loads[3].wait()
    loads[4].wait()
    lx_src[...] = jnp.full((1, 128), length_ref[0].astype(F32), F32)
    word(4)
    for p, offsets in enumerate(QUERY_OFFSETS):
        drain(qx_dst.at[p], recv_sems.at[1 + p])
        qz_src[pl.ds(4 * p, 4)] = qx_src[p, x] + qx_dst[p, 0] + qx_dst[p, 1] + qx_dst[p, 2]
        for k in offsets:
            send(
                qz_src.at[(k + 2) % CHUNKS],
                qz_dst.at[k - 1],
                send_sems.at[4],
                recv_sems.at[4],
                device(k, 0),
            )
        if p == 0:
            drain(sx_dst, recv_sems.at[0])
            sz_src[...] = sx_src[...] + sx_dst[0] + sx_dst[1] + sx_dst[2]
            for k in FAR_FIRST:
                send(sz_src, sz_dst.at[k - 1], send_sems.at[3], recv_sems.at[3], device(k, 0))
            at_end(3, sz_dst)
    at_end(4, qz_dst)
    x_same(lx_src, lx_dst, 5)
    x_same(key, kx_dst, 6)
    x_same(value, vx_dst, 7)
    mine = lax.rem(z, CHUNKS)
    slot = x * CHUNKS + mine
    drain(sz_dst, recv_sems.at[3])
    squares = jnp.sum(sz_dst[...], axis=0) + sz_src[...]
    scale = lax.rsqrt(row_column(squares, 16 * lax.rem(mine, 4)) / D + EPSILON)
    drain(qz_dst, recv_sems.at[4])
    total = qz_src[2] + jnp.sum(qz_dst[...], axis=0)
    q_all[mine] = (scale * total).astype(BF16)
    for dz in NEAR_Z:
        send(q_all.at[mine], q_all.at[mine], send_sems.at[8], recv_sems.at[8], device(dz, 0))
    at_end(8, q_all.at[pl.ds(0, CHUNKS - 1)])
    loads[6].wait()
    for j in range(NX):
        for h in range(2):
            at = (2 * j + h) * HD
            w_turned[pl.ds(HD * h, HD), pl.ds(HD * j, HD)] = jnp.transpose(
                wout[at : at + HD].astype(F32)
            ).astype(BF16)
    drain(lx_dst, recv_sems.at[5])
    drain(kx_dst, recv_sems.at[6])
    drain(vx_dst, recv_sems.at[7])
    keys = [key] + [kx_dst.at[k] for k in range(NX - 1)]
    values = [value] + [vx_dst.at[k] for k in range(NX - 1)]
    lengths = [lx_src] + [lx_dst.at[k] for k in range(NX - 1)]
    for n in range(NX):
        v_turned[n] = jnp.transpose(values[n][...].astype(F32)).astype(BF16)
    drain(q_all.at[pl.ds(0, CHUNKS - 1)], recv_sems.at[8])

    queries = q_all[...].reshape(CHUNKS * 16, HD)
    token = lax.broadcasted_iota(jnp.int32, (BLOCK, 128), 0).astype(F32)
    found = []
    for n in range(NX):
        scores = lax.dot_general(
            keys[n][...], queries, (((1,), (1,)), ((), ())), preferred_element_type=F32
        ) * (1.0 / math.sqrt(HD))
        scores = jnp.where(token < lengths[n][...], scores, MASKED)
        maxima = jnp.max(scores, axis=0, keepdims=True)
        weights = jnp.exp(scores - maxima)
        totals = jnp.sum(weights, axis=0, keepdims=True)
        numerators = jnp.dot(v_turned[n], weights.astype(BF16), preferred_element_type=F32)
        found.append((maxima, totals, numerators))
    summit = functools.reduce(jnp.maximum, [piece[0] for piece in found])
    factors = [jnp.exp(piece[0] - summit) for piece in found]
    tz_src[0] = summit
    tz_src[1] = sum(factor * piece[1] for factor, piece in zip(factors, found))
    merged = sum(factor * piece[2] for factor, piece in zip(factors, found))
    for i in range(CHUNKS):
        az_src[i] = merged[16 * i : 16 * i + 16].astype(BF16)
    z_scatter(az_src, az_dst, 10, tz_src, tz_dst, 9)
    drain(tz_dst, recv_sems.at[9])
    own = tz_src[0]
    others = tz_dst[:, 0]
    summit = jnp.maximum(own, jnp.max(others, axis=0))
    own_factor = jnp.exp(own - summit)
    factors = jnp.exp(others - summit)
    total = own_factor * tz_src[1] + jnp.sum(factors * tz_dst[:, 1], axis=0)
    drain(az_dst, recv_sems.at[10])
    merged = own_factor * az_src[mine].astype(F32) + jnp.sum(
        factors * az_dst[...].astype(F32), axis=0
    )
    a_all[slot] = (merged / total).astype(BF16)
    near_gather(a_all, 11)

    both = jnp.dot(
        w_turned[...], a_all[...].reshape(NX * HD, 128), preferred_element_type=F32
    )
    projected = jnp.transpose(both[:HD, :ROWS] + both[HD:, ROWS:])

    def tp_sum(part, whole, at, sems):
        whole[tp] = part.astype(BF16)
        for k in (4, 5, 2, 3, 6, 7, 1):
            send(whole.at[tp], whole.at[tp], send_sems.at[at], sems.at[tp], (ctx, t_of(k)))
        if at == LAST:
            finish()
        for k in (1, 7, 6, 3, 2, 5, 4):
            source = t_of(k)
            drain(whole.at[source], sems.at[source])
        if at == LAST:
            drain(whole.at[pl.ds(0, NT - 1)], send_sems.at[at])
        else:
            at_end(at, whole.at[pl.ds(0, NT - 1)])
        total = whole[0].astype(F32)
        for source in range(1, NT):
            total = total + whole[source].astype(F32)
        return total

    residual = hidden[...].astype(F32) + tp_sum(projected, p_all, 12, p_sems)

    loads[5].wait()
    second = (residual * ffn_gain[...]).astype(BF16)
    loads[7].wait()
    loads[8].wait()
    order = FAR_FIRST + (0,)
    ux_row = lane_row(jnp.sum(residual * residual, axis=1, keepdims=True))
    for p, (start, size) in enumerate(PIECES):
        for s in range(size):
            block = jnp.minimum(z_of(order[start + s]), FF_BLOCKS - 1)
            columns = pl.ds(pl.multiple_of(block * 128, 128), 128)
            pair = jnp.concatenate([wgate[:, columns], wup[:, columns]], axis=1)
            part = jnp.dot(second, pair, preferred_element_type=F32).astype(BF16)
            for j in range(NX):
                fx_src[NX * start + j * size + s, 0] = part[16 * j : 16 * j + 16, :128]
                fx_src[NX * start + j * size + s, 1] = part[16 * j : 16 * j + 16, 128:]
        for k in range(1, NX):
            send(
                fx_src.at[pl.ds(NX * start + x_of(k) * size, size)],
                fx_dst.at[pl.ds((NX - 1) * start + (k - 1) * size, size)],
                send_sems.at[14 + p],
                recv_sems.at[14 + p],
                device(0, k),
            )
        at_end(14 + p, fx_dst.at[pl.ds((NX - 1) * start, (NX - 1) * size)])
        if p == 0:
            ux_src[...] = ux_row
            x_same(ux_src, ux_dst, 13)
    for p, (start, size) in enumerate(PIECES):
        drain(fx_dst.at[pl.ds((NX - 1) * start, (NX - 1) * size)], recv_sems.at[14 + p])
        piece = fx_src[pl.ds(NX * start + x * size, size)].astype(F32)
        for k in range(1, NX):
            at = (NX - 1) * start + (k - 1) * size
            piece = piece + fx_dst[at : at + size].astype(F32)
        fz_src[start : start + size] = piece.astype(BF16)
        if p == 1:
            drain(ux_dst, recv_sems.at[13])
            uz_src[...] = ux_src[...] + ux_dst[0] + ux_dst[1] + ux_dst[2]
            for k in FAR_FIRST:
                send(uz_src, uz_dst.at[k - 1], send_sems.at[18], recv_sems.at[18], device(k, 0))
            at_end(18, uz_dst)
        for s in range(size):
            k = order[start + s]
            if k == 0:
                continue

            @pl.when(z_of(k) < FF_BLOCKS)
            def _():
                send(
                    fz_src.at[start + s],
                    fz_dst.at[k - 1],
                    send_sems.at[19],
                    recv_sems.at[19],
                    device(k, 0),
                )

    reduces = z < FF_BLOCKS
    at_end(19, fz_dst.at[pl.ds(0, FF_BLOCKS - 1)], reduces)
    at_end(19, fz_dst.at[pl.ds(0, FF_BLOCKS)], jnp.logical_not(reduces))
    drain(uz_dst, recv_sems.at[18])
    squares = jnp.sum(uz_dst[...], axis=0) + uz_src[...]
    scale = lax.rsqrt(row_column(squares, 16 * x) / D + EPSILON)

    def x_forward(block):
        for k in (2, 1, 3):
            send(
                f_all.at[x, block],
                f_all.at[x, block],
                send_sems.at[21],
                recv_sems.at[21],
                device(0, k),
            )

    @pl.when(reduces)
    def _():
        drain(fz_dst, recv_sems.at[19])
        both = fz_src[NZ - 1].astype(F32) + jnp.sum(fz_dst[...].astype(F32), axis=0)
        gate = scale * both[0]
        up = scale * both[1]
        f_all[x, z] = (gate / (1.0 + jnp.exp(-gate)) * up).astype(BF16)
        for k in FAR_FIRST:
            send(f_all.at[x, z], f_all.at[x, z], send_sems.at[20], f_gather_sems.at[z], device(k, 0))
        x_forward(z)

    at_end(20, az_dst, reduces)

    for k in reversed(FAR_FIRST):
        block = z_of(k)

        @pl.when(block < FF_BLOCKS)
        def _():
            drain(f_all.at[x, block], f_gather_sems.at[block])
            x_forward(block)

    drain(f_all.at[pl.ds(0, NX - 1)], recv_sems.at[21])
    at_end(21, f_all.at[pl.ds(0, NX - 1)])

    loads[9].wait()
    activated = jnp.concatenate(
        [f_all[:, b].reshape(ROWS, 128) for b in range(FF_BLOCKS)], axis=1
    )
    lowered = jnp.dot(activated, wdown[...], preferred_element_type=F32)
    result = residual + tp_sum(lowered, d_all, 22, d_sems)
    out_ref[...] = result.astype(BF16)


def body(
    hidden_in,
    attn_gain,
    w_query,
    key_cache,
    value_cache,
    block_lengths,
    question_length,
    w_out,
    ffn_gain,
    w_gate,
    w_up,
    w_down,
):
    operands = (
        hidden_in,
        attn_gain.reshape(1, -1),
        ffn_gain.reshape(1, -1),
        w_query,
        key_cache,
        value_cache,
        w_out,
        w_gate,
        w_up,
        w_down,
    )
    chunk = (16, 128)
    row = (1, 128)
    dma = pltpu.SemaphoreType.DMA
    scratch = [pltpu.VMEM(a.shape, a.dtype) for a in operands]
    scratch += [dma((len(operands),)), dma((23,)), dma((23,))]
    scratch += [
        pltpu.VMEM((2, NX, 4) + chunk, F32),
        pltpu.VMEM((2, NX - 1, 4) + chunk, F32),
        pltpu.VMEM((CHUNKS,) + chunk, F32),
        pltpu.VMEM((NZ - 1,) + chunk, F32),
        pltpu.VMEM((CHUNKS,) + chunk, BF16),
        pltpu.VMEM(row, F32),
        pltpu.VMEM((NX - 1,) + row, F32),
        pltpu.VMEM(row, F32),
        pltpu.VMEM((NZ - 1,) + row, F32),
        pltpu.VMEM((NX - 1, BLOCK, HD), BF16),
        pltpu.VMEM((NX - 1, BLOCK, HD), BF16),
        pltpu.VMEM(row, F32),
        pltpu.VMEM((NX - 1,) + row, F32),
        pltpu.VMEM((NX, HD, BLOCK), BF16),
        pltpu.VMEM((2 * HD, NX * HD), BF16),
        pltpu.VMEM((CHUNKS,) + chunk, BF16),
        pltpu.VMEM((NZ - 1,) + chunk, BF16),
        pltpu.VMEM((NX * CHUNKS,) + chunk, BF16),
        pltpu.VMEM((2,) + row, F32),
        pltpu.VMEM((NZ - 1, 2) + row, F32),
        pltpu.VMEM((NT, ROWS, 128), BF16),
        pltpu.VMEM((NX * NZ, 2) + chunk, BF16),
        pltpu.VMEM(((NX - 1) * NZ, 2) + chunk, BF16),
        pltpu.VMEM((NZ, 2) + chunk, BF16),
        pltpu.VMEM((NZ - 1, 2) + chunk, BF16),
        pltpu.VMEM((NX, FF_BLOCKS) + chunk, BF16),
        pltpu.VMEM(row, F32),
        pltpu.VMEM((NX - 1,) + row, F32),
        pltpu.VMEM(row, F32),
        pltpu.VMEM((NZ - 1,) + row, F32),
        pltpu.VMEM((NT, ROWS, 128), BF16),
        pltpu.SemaphoreType.REGULAR((2,)),
        dma((FF_BLOCKS,)),
        dma((NT,)),
        dma((NT,)),
    ]
    result = pl.pallas_call(
        kernel,
        out_shape=pltpu.VMEM(hidden_in.shape, BF16),
        in_specs=[pl.BlockSpec(memory_space=pltpu.SMEM)]
        + [pl.BlockSpec(memory_space=pl.ANY)] * len(operands),
        out_specs=pl.BlockSpec(memory_space=pltpu.VMEM),
        scratch_shapes=scratch,
        compiler_params=pltpu.CompilerParams(
            collective_id=0, has_side_effects=True, vmem_limit_bytes=60 * 1024 * 1024
        ),
    )(block_lengths, *operands)
    present = jnp.arange(ROWS)[:, None] < question_length[0]
    return jnp.where(present, result, jnp.zeros_like(result))


def solution(mesh):
    placed = (
        P(None, "ctx"),
        P("ctx"),
        P("ctx", "tp"),
        P("ctx", "tp"),
        P("ctx", "tp"),
        P("ctx"),
        P(),
        P("tp", "ctx"),
        P("ctx"),
        P("ctx", "tp"),
        P("ctx", "tp"),
        P("tp", "ctx"),
    )
    return jax.shard_map(
        body, mesh=mesh, in_specs=placed, out_specs=P(None, "ctx"), check_vma=False
    )
```

```python
import functools
import math

import jax
import jax.numpy as jnp
from jax import lax
from jax.experimental import pallas as pl
from jax.experimental.pallas import tpu as pltpu
from jax.sharding import PartitionSpec as P

D = 8192
HD = 128
EPSILON = 1e-05
MASKED = -1e30
LAST = 22
NX = 4
NZ = 16
NT = 8
ROWS = 64
BLOCK = 512
CHUNKS = 8
FF_BLOCKS = 14
PIECES = ((0, 2), (2, 3), (5, 5), (10, 6))
FAR_FIRST = (8, 7, 9, 6, 10, 5, 11, 4, 12, 3, 13, 2, 14, 1, 15)
QUERY_OFFSETS = ((8, 7, 9, 6, 14, 1, 15), (10, 5, 11, 4, 12, 3, 13, 2))
NEAR_Z = (4, 3, 13, 2, 14, 1, 15)
NEAR = tuple(
    (dz % NZ, dx)
    for dz in (4, 3, -3, 2, -2, 1, -1, 0)
    for dx in (2, 1, 3, 0)
    if (dz, dx) != (0, 0)
)
MESH = pl.DeviceIdType.MESH
F32 = jnp.float32
BF16 = jnp.bfloat16


def lane_row(column):
    shape = (column.shape[0], 128)
    same = lax.broadcasted_iota(jnp.int32, shape, 0) == lax.broadcasted_iota(jnp.int32, shape, 1)
    return jnp.sum(jnp.where(same, jnp.broadcast_to(column, shape), 0.0), axis=0, keepdims=True)


def row_column(row, base):
    shape = (16, 128)
    same = lax.broadcasted_iota(jnp.int32, shape, 0) + base == lax.broadcasted_iota(
        jnp.int32, shape, 1
    )
    return jnp.sum(jnp.where(same, jnp.broadcast_to(row, shape), 0.0), axis=1, keepdims=True)


def kernel(
    length_hbm,
    question_hbm,
    hidden_hbm,
    attn_gain_hbm,
    ffn_gain_hbm,
    wq_hbm,
    key_hbm,
    value_hbm,
    wout_hbm,
    wgate_hbm,
    wup_hbm,
    wdown_hbm,
    out_ref,
    length_ref,
    question_ref,
    hidden,
    attn_gain,
    ffn_gain,
    wq,
    key,
    value,
    wout,
    wgate,
    wup,
    wdown,
    load_sems,
    send_sems,
    recv_sems,
    qx_src,
    qx_dst,
    qz_src,
    qz_dst,
    q_all,
    sx_src,
    sx_dst,
    sz_src,
    sz_dst,
    kx_dst,
    vx_dst,
    lx_src,
    lx_dst,
    v_turned,
    w_turned,
    az_src,
    az_dst,
    a_all,
    tz_src,
    tz_dst,
    p_all,
    fx_src,
    fx_dst,
    fz_src,
    fz_dst,
    f_all,
    ux_src,
    ux_dst,
    uz_src,
    uz_dst,
    d_all,
    word_sems,
    f_gather_sems,
    p_sems,
    d_sems,
):
    ctx = lax.axis_index("ctx")
    tp = lax.axis_index("tp")
    x = lax.rem(ctx, NX)
    z = lax.div(ctx, NX)

    def x_of(k):
        return lax.rem(x + k, NX)

    def z_of(k):
        return lax.rem(z + k, NZ)

    def t_of(k):
        return lax.rem(tp + k, NT)

    def device(dz, dx):
        return (z_of(dz) * NX + x_of(dx), tp)

    sources = (
        hidden_hbm,
        attn_gain_hbm,
        wq_hbm,
        key_hbm,
        value_hbm,
        ffn_gain_hbm,
        wout_hbm,
        wgate_hbm,
        wup_hbm,
        wdown_hbm,
        length_hbm,
        question_hbm,
    )
    targets = (
        hidden,
        attn_gain,
        wq,
        key,
        value,
        ffn_gain,
        wout,
        wgate,
        wup,
        wdown,
        length_ref,
        question_ref,
    )
    loads = [
        pltpu.make_async_copy(source, target, load_sems.at[at])
        for at, (source, target) in enumerate(zip(sources, targets))
    ]
    barrier = pltpu.get_barrier_semaphore()
    for k in (2, 14, 1, 15):
        pl.semaphore_signal(barrier, inc=1, device_id=device(k, 0), device_id_type=MESH)
    for k in range(1, NX):
        pl.semaphore_signal(barrier, inc=1, device_id=device(0, k), device_id_type=MESH)
    for k in range(1, NT):
        pl.semaphore_signal(barrier, inc=1, device_id=(ctx, t_of(k)), device_id_type=MESH)

    for load in loads:
        load.start()

    def pass_on(step):
        for k in (step, NZ - step):
            pl.semaphore_signal(
                word_sems.at[step // 4], inc=1, device_id=device(k, 0), device_id_type=MESH
            )

    def word(step):
        pl.semaphore_wait(word_sems.at[step // 4], 2)

    def send(source, target, send_sem, recv_sem, peer):
        pltpu.make_async_remote_copy(
            src_ref=source,
            dst_ref=target,
            send_sem=send_sem,
            recv_sem=recv_sem,
            device_id=peer,
            device_id_type=MESH,
        ).start()

    def drain(ref, sem):
        pltpu.make_async_copy(ref, ref, sem).wait()

    pending = []

    def at_end(sem_at, ref, condition=None):
        pending.append((sem_at, ref, condition))

    def finish():
        for sem_at, ref, condition in pending:
            if condition is None:
                drain(ref, send_sems.at[sem_at])
            else:
                pl.when(condition)(functools.partial(drain, ref, send_sems.at[sem_at]))

    def x_scatter(source, target, at):
        for k in range(1, NX):
            send(source.at[x_of(k)], target.at[k - 1], send_sems.at[at], recv_sems.at[at], device(0, k))
        at_end(at, target)

    def x_same(source, target, at):
        for k in range(1, NX):
            send(source, target.at[k - 1], send_sems.at[at], recv_sems.at[at], device(0, k))
        at_end(at, target)

    def z_scatter(source, target, at, row_source, row_target, row_at):
        for k in FAR_FIRST:
            send(
                row_source,
                row_target.at[k - 1],
                send_sems.at[row_at],
                recv_sems.at[row_at],
                device(k, 0),
            )
            send(
                source.at[lax.rem(z + k, CHUNKS)],
                target.at[k - 1],
                send_sems.at[at],
                recv_sems.at[at],
                device(k, 0),
            )
        at_end(row_at, row_target)
        at_end(at, target)

    def near_gather(whole, at):
        own = x * CHUNKS + lax.rem(z, CHUNKS)
        for dz, dx in NEAR:
            send(whole.at[own], whole.at[own], send_sems.at[at], recv_sems.at[at], device(dz, dx))
        rest = whole.at[pl.ds(0, NX * CHUNKS - 1)]
        drain(rest, recv_sems.at[at])
        at_end(at, rest)

    loads[0].wait()
    loads[1].wait()
    stream = hidden[...].astype(F32)
    normed = (stream * attn_gain[...]).astype(BF16)
    loads[2].wait()
    query_part = jnp.dot(normed, wq[...], preferred_element_type=F32)
    for i in range(CHUNKS):
        place = lax.rem(i - z + NZ + 2, CHUNKS)
        for j in range(NX):
            column = (2 * j + i // 4) * HD
            row = 16 * (i % 4)
            qx_src[lax.div(place, 4), j, lax.rem(place, 4)] = query_part[
                row : row + 16, column : column + HD
            ]
    pl.semaphore_wait(barrier, 4 + NX - 1 + NT - 1)
    pass_on(2)

    for p in range(2):
        x_scatter(qx_src.at[p], qx_dst.at[p], 1 + p)
    sx_src[...] = lane_row(jnp.sum(stream * stream, axis=1, keepdims=True))
    x_same(sx_src, sx_dst, 0)
    word(2)
    pass_on(4)
    loads[3].wait()
    loads[4].wait()
    loads[10].wait()
    lx_src[...] = jnp.full((1, 128), length_ref[0].astype(F32), F32)
    word(4)
    for p, offsets in enumerate(QUERY_OFFSETS):
        drain(qx_dst.at[p], recv_sems.at[1 + p])
        qz_src[pl.ds(4 * p, 4)] = qx_src[p, x] + qx_dst[p, 0] + qx_dst[p, 1] + qx_dst[p, 2]
        for k in offsets:
            send(
                qz_src.at[(k + 2) % CHUNKS],
                qz_dst.at[k - 1],
                send_sems.at[4],
                recv_sems.at[4],
                device(k, 0),
            )
        if p == 0:
            drain(sx_dst, recv_sems.at[0])
            sz_src[...] = sx_src[...] + sx_dst[0] + sx_dst[1] + sx_dst[2]
            for k in FAR_FIRST:
                send(sz_src, sz_dst.at[k - 1], send_sems.at[3], recv_sems.at[3], device(k, 0))
            at_end(3, sz_dst)
    at_end(4, qz_dst)
    x_same(lx_src, lx_dst, 5)
    x_same(key, kx_dst, 6)
    x_same(value, vx_dst, 7)
    mine = lax.rem(z, CHUNKS)
    slot = x * CHUNKS + mine
    drain(sz_dst, recv_sems.at[3])
    squares = jnp.sum(sz_dst[...], axis=0) + sz_src[...]
    scale = lax.rsqrt(row_column(squares, 16 * lax.rem(mine, 4)) / D + EPSILON)
    drain(qz_dst, recv_sems.at[4])
    total = qz_src[2] + jnp.sum(qz_dst[...], axis=0)
    q_all[mine] = (scale * total).astype(BF16)
    for dz in NEAR_Z:
        send(q_all.at[mine], q_all.at[mine], send_sems.at[8], recv_sems.at[8], device(dz, 0))
    at_end(8, q_all.at[pl.ds(0, CHUNKS - 1)])
    loads[6].wait()
    for j in range(NX):
        for h in range(2):
            at = (2 * j + h) * HD
            w_turned[pl.ds(HD * h, HD), pl.ds(HD * j, HD)] = jnp.transpose(
                wout[at : at + HD].astype(F32)
            ).astype(BF16)
    drain(lx_dst, recv_sems.at[5])
    drain(kx_dst, recv_sems.at[6])
    drain(vx_dst, recv_sems.at[7])
    keys = [key] + [kx_dst.at[k] for k in range(NX - 1)]
    values = [value] + [vx_dst.at[k] for k in range(NX - 1)]
    lengths = [lx_src] + [lx_dst.at[k] for k in range(NX - 1)]
    for n in range(NX):
        v_turned[n] = jnp.transpose(values[n][...].astype(F32)).astype(BF16)
    drain(q_all.at[pl.ds(0, CHUNKS - 1)], recv_sems.at[8])

    queries = q_all[...].reshape(CHUNKS * 16, HD)
    token = lax.broadcasted_iota(jnp.int32, (BLOCK, 128), 0).astype(F32)
    found = []
    for n in range(NX):
        scores = lax.dot_general(
            keys[n][...], queries, (((1,), (1,)), ((), ())), preferred_element_type=F32
        ) * (1.0 / math.sqrt(HD))
        scores = jnp.where(token < lengths[n][...], scores, MASKED)
        maxima = jnp.max(scores, axis=0, keepdims=True)
        weights = jnp.exp(scores - maxima)
        totals = jnp.sum(weights, axis=0, keepdims=True)
        numerators = jnp.dot(v_turned[n], weights.astype(BF16), preferred_element_type=F32)
        found.append((maxima, totals, numerators))
    summit = functools.reduce(jnp.maximum, [piece[0] for piece in found])
    factors = [jnp.exp(piece[0] - summit) for piece in found]
    tz_src[0] = summit
    tz_src[1] = sum(factor * piece[1] for factor, piece in zip(factors, found))
    merged = sum(factor * piece[2] for factor, piece in zip(factors, found))
    for i in range(CHUNKS):
        az_src[i] = merged[16 * i : 16 * i + 16].astype(BF16)
    z_scatter(az_src, az_dst, 10, tz_src, tz_dst, 9)
    drain(tz_dst, recv_sems.at[9])
    own = tz_src[0]
    others = tz_dst[:, 0]
    summit = jnp.maximum(own, jnp.max(others, axis=0))
    own_factor = jnp.exp(own - summit)
    factors = jnp.exp(others - summit)
    total = own_factor * tz_src[1] + jnp.sum(factors * tz_dst[:, 1], axis=0)
    drain(az_dst, recv_sems.at[10])
    merged = own_factor * az_src[mine].astype(F32) + jnp.sum(
        factors * az_dst[...].astype(F32), axis=0
    )
    a_all[slot] = (merged / total).astype(BF16)
    near_gather(a_all, 11)

    both = jnp.dot(
        w_turned[...], a_all[...].reshape(NX * HD, 128), preferred_element_type=F32
    )
    projected = jnp.transpose(both[:HD, :ROWS] + both[HD:, ROWS:])

    def tp_sum(part, whole, at, sems):
        whole[tp] = part.astype(BF16)
        for k in (4, 5, 2, 3, 6, 7, 1):
            send(whole.at[tp], whole.at[tp], send_sems.at[at], sems.at[tp], (ctx, t_of(k)))
        if at == LAST:
            finish()
        for k in (1, 7, 6, 3, 2, 5, 4):
            source = t_of(k)
            drain(whole.at[source], sems.at[source])
        if at == LAST:
            drain(whole.at[pl.ds(0, NT - 1)], send_sems.at[at])
        else:
            at_end(at, whole.at[pl.ds(0, NT - 1)])
        total = whole[0].astype(F32)
        for source in range(1, NT):
            total = total + whole[source].astype(F32)
        return total

    residual = hidden[...].astype(F32) + tp_sum(projected, p_all, 12, p_sems)

    loads[5].wait()
    second = (residual * ffn_gain[...]).astype(BF16)
    loads[7].wait()
    loads[8].wait()
    order = FAR_FIRST + (0,)
    ux_row = lane_row(jnp.sum(residual * residual, axis=1, keepdims=True))
    for p, (start, size) in enumerate(PIECES):
        for s in range(size):
            block = jnp.minimum(z_of(order[start + s]), FF_BLOCKS - 1)
            columns = pl.ds(pl.multiple_of(block * 128, 128), 128)
            pair = jnp.concatenate([wgate[:, columns], wup[:, columns]], axis=1)
            part = jnp.dot(second, pair, preferred_element_type=F32).astype(BF16)
            for j in range(NX):
                fx_src[NX * start + j * size + s, 0] = part[16 * j : 16 * j + 16, :128]
                fx_src[NX * start + j * size + s, 1] = part[16 * j : 16 * j + 16, 128:]
        for k in range(1, NX):
            send(
                fx_src.at[pl.ds(NX * start + x_of(k) * size, size)],
                fx_dst.at[pl.ds((NX - 1) * start + (k - 1) * size, size)],
                send_sems.at[14 + p],
                recv_sems.at[14 + p],
                device(0, k),
            )
        at_end(14 + p, fx_dst.at[pl.ds((NX - 1) * start, (NX - 1) * size)])
        if p == 0:
            ux_src[...] = ux_row
            x_same(ux_src, ux_dst, 13)
    for p, (start, size) in enumerate(PIECES):
        drain(fx_dst.at[pl.ds((NX - 1) * start, (NX - 1) * size)], recv_sems.at[14 + p])
        piece = fx_src[pl.ds(NX * start + x * size, size)].astype(F32)
        for k in range(1, NX):
            at = (NX - 1) * start + (k - 1) * size
            piece = piece + fx_dst[at : at + size].astype(F32)
        fz_src[start : start + size] = piece.astype(BF16)
        if p == 1:
            drain(ux_dst, recv_sems.at[13])
            uz_src[...] = ux_src[...] + ux_dst[0] + ux_dst[1] + ux_dst[2]
            for k in FAR_FIRST:
                send(uz_src, uz_dst.at[k - 1], send_sems.at[18], recv_sems.at[18], device(k, 0))
            at_end(18, uz_dst)
        for s in range(size):
            k = order[start + s]
            if k == 0:
                continue

            @pl.when(z_of(k) < FF_BLOCKS)
            def _():
                send(
                    fz_src.at[start + s],
                    fz_dst.at[k - 1],
                    send_sems.at[19],
                    recv_sems.at[19],
                    device(k, 0),
                )

    reduces = z < FF_BLOCKS
    at_end(19, fz_dst.at[pl.ds(0, FF_BLOCKS - 1)], reduces)
    at_end(19, fz_dst.at[pl.ds(0, FF_BLOCKS)], jnp.logical_not(reduces))
    drain(uz_dst, recv_sems.at[18])
    squares = jnp.sum(uz_dst[...], axis=0) + uz_src[...]
    scale = lax.rsqrt(row_column(squares, 16 * x) / D + EPSILON)

    def x_forward(block):
        for k in (2, 1, 3):
            send(
                f_all.at[x, block],
                f_all.at[x, block],
                send_sems.at[21],
                recv_sems.at[21],
                device(0, k),
            )

    @pl.when(reduces)
    def _():
        drain(fz_dst, recv_sems.at[19])
        both = fz_src[NZ - 1].astype(F32) + jnp.sum(fz_dst[...].astype(F32), axis=0)
        gate = scale * both[0]
        up = scale * both[1]
        f_all[x, z] = (gate / (1.0 + jnp.exp(-gate)) * up).astype(BF16)
        for k in FAR_FIRST:
            send(f_all.at[x, z], f_all.at[x, z], send_sems.at[20], f_gather_sems.at[z], device(k, 0))
        x_forward(z)

    at_end(20, az_dst, reduces)

    for k in reversed(FAR_FIRST):
        block = z_of(k)

        @pl.when(block < FF_BLOCKS)
        def _():
            drain(f_all.at[x, block], f_gather_sems.at[block])
            x_forward(block)

    drain(f_all.at[pl.ds(0, NX - 1)], recv_sems.at[21])
    at_end(21, f_all.at[pl.ds(0, NX - 1)])

    loads[9].wait()
    activated = jnp.concatenate(
        [f_all[:, b].reshape(ROWS, 128) for b in range(FF_BLOCKS)], axis=1
    )
    lowered = jnp.dot(activated, wdown[...], preferred_element_type=F32)
    result = residual + tp_sum(lowered, d_all, 22, d_sems)
    loads[11].wait()
    present = lax.broadcasted_iota(jnp.int32, result.shape, 0) < question_ref[0]
    out_ref[...] = jnp.where(present, result, 0.0).astype(BF16)


def body(
    hidden_in,
    attn_gain,
    w_query,
    key_cache,
    value_cache,
    block_lengths,
    question_length,
    w_out,
    ffn_gain,
    w_gate,
    w_up,
    w_down,
):
    operands = (
        hidden_in,
        attn_gain.reshape(1, -1),
        ffn_gain.reshape(1, -1),
        w_query,
        key_cache,
        value_cache,
        w_out,
        w_gate,
        w_up,
        w_down,
    )
    chunk = (16, 128)
    row = (1, 128)
    dma = pltpu.SemaphoreType.DMA
    scratch = [pltpu.SMEM((1,), jnp.int32)] * 2
    scratch += [pltpu.VMEM(a.shape, a.dtype) for a in operands]
    scratch += [dma((2 + len(operands),)), dma((23,)), dma((23,))]
    scratch += [
        pltpu.VMEM((2, NX, 4) + chunk, F32),
        pltpu.VMEM((2, NX - 1, 4) + chunk, F32),
        pltpu.VMEM((CHUNKS,) + chunk, F32),
        pltpu.VMEM((NZ - 1,) + chunk, F32),
        pltpu.VMEM((CHUNKS,) + chunk, BF16),
        pltpu.VMEM(row, F32),
        pltpu.VMEM((NX - 1,) + row, F32),
        pltpu.VMEM(row, F32),
        pltpu.VMEM((NZ - 1,) + row, F32),
        pltpu.VMEM((NX - 1, BLOCK, HD), BF16),
        pltpu.VMEM((NX - 1, BLOCK, HD), BF16),
        pltpu.VMEM(row, F32),
        pltpu.VMEM((NX - 1,) + row, F32),
        pltpu.VMEM((NX, HD, BLOCK), BF16),
        pltpu.VMEM((2 * HD, NX * HD), BF16),
        pltpu.VMEM((CHUNKS,) + chunk, BF16),
        pltpu.VMEM((NZ - 1,) + chunk, BF16),
        pltpu.VMEM((NX * CHUNKS,) + chunk, BF16),
        pltpu.VMEM((2,) + row, F32),
        pltpu.VMEM((NZ - 1, 2) + row, F32),
        pltpu.VMEM((NT, ROWS, 128), BF16),
        pltpu.VMEM((NX * NZ, 2) + chunk, BF16),
        pltpu.VMEM(((NX - 1) * NZ, 2) + chunk, BF16),
        pltpu.VMEM((NZ, 2) + chunk, BF16),
        pltpu.VMEM((NZ - 1, 2) + chunk, BF16),
        pltpu.VMEM((NX, FF_BLOCKS) + chunk, BF16),
        pltpu.VMEM(row, F32),
        pltpu.VMEM((NX - 1,) + row, F32),
        pltpu.VMEM(row, F32),
        pltpu.VMEM((NZ - 1,) + row, F32),
        pltpu.VMEM((NT, ROWS, 128), BF16),
        pltpu.SemaphoreType.REGULAR((2,)),
        dma((FF_BLOCKS,)),
        dma((NT,)),
        dma((NT,)),
    ]
    return pl.pallas_call(
        kernel,
        out_shape=pltpu.VMEM(hidden_in.shape, BF16),
        in_specs=[pl.BlockSpec(memory_space=pl.ANY)] * (2 + len(operands)),
        out_specs=pl.BlockSpec(memory_space=pltpu.VMEM),
        scratch_shapes=scratch,
        compiler_params=pltpu.CompilerParams(
            collective_id=0, has_side_effects=True, vmem_limit_bytes=60 * 1024 * 1024
        ),
    )(block_lengths, question_length, *operands)


def solution(mesh):
    placed = (
        P(None, "ctx"),
        P("ctx"),
        P("ctx", "tp"),
        P("ctx", "tp"),
        P("ctx", "tp"),
        P("ctx"),
        P(),
        P("tp", "ctx"),
        P("ctx"),
        P("ctx", "tp"),
        P("ctx", "tp"),
        P("tp", "ctx"),
    )
    return jax.shard_map(
        body, mesh=mesh, in_specs=placed, out_specs=P(None, "ctx"), check_vma=False
    )
```
